256 devices in a mesh: lat: 32 (over y, x, core), src: 8 (over z).
Axes of the slice: x: 4, y: 4, z: 8, core: 2. Of those that a mesh axis runs over, the one named last changes fastest.
Arguments:
- swath: bfloat16 [8, 1024, 616, 128], P('src', 'lat'), may hold values from -6 to 6
- tile_band: int32 [8, 1024, 1], P('src', 'lat'), may hold values from 0 to 31; in each aligned block of 32 rows (0 to 31, 32 to 63, ..., all dimensions but the last counted through in order) at most 2 rows name the same one
- tile_patch: int32 [8, 1024], P('src', 'lat'), may hold values from 0 to 31
- fp_pos: bfloat16 [8, 1024, 2, 128], P('src', 'lat'), may hold values from 0 to 24, as said below
- conv_weight: bfloat16 [8, 4, 4, 616, 512], P('src', None, None, None, 'lat'), may hold values from -0.0625 to 0.0625
- conv_bias: float32 [8, 512], P('src'), may hold values from -6 to 6
- norm_gain: float32 [512], replicated, may hold values from 0.1 to 1.9
- latents: float32 [4, 512], replicated, may hold values from -200 to 200
- kv_weight: bfloat16 [512, 1024], replicated, may hold values from -0.25 to 0.25
- out_weight: bfloat16 [512, 512], replicated, may hold values from -0.25 to 0.25
Outputs:
- latent_out: float32 [1024, 4, 512], P(('lat', 'src'))
The draws below stay inside these ranges and needn't reach their ends.
Inputs may be any that keep to these rules, and one draw needn't show every extreme that they name: `tile_band`: among the tiles of one source on one index of lat no band is named more than 2 times; some band is named exactly 2 times. `fp_pos`: the first of the two rows lies in [0, 8), the second in [0, 24).
All inputs are finite; a program needn't handle non-finite values.
Results may differ from the reference program's by a relative error of at most 0.035.
Values may be sent and summed in bfloat16 or wider, within the bound.
No kernel may reach another device: no remote copies, remote signals or barrier semaphores. Data moves between devices by JAX's collectives and lax.ppermute only.
A program may use at most 192 MiB of HBM per device.

```python
import math
import jax
import jax.numpy as jnp
import numpy as np
from jax import lax

CH = 616
FP = 128
D = 512
HEADS = 8
HD = 64
PH = 8
PW = 24
KS = 4
TPS = 12
LEVELS = 4
TILE_DEV = 32
PATCH_DEV = 32
CAP = 2
SOURCES = 8
TILES = 1024
PATCHES = 1024
N_LAT = 32


def draw_fp_pos(key, part):
    key = jax.random.fold_in(key, 3)
    unit = jax.random.uniform(key, (SOURCES, TILES, 2, FP), jnp.float32)
    extent = jnp.array([PH, PW], jnp.float32).reshape(1, 1, 2, 1)
    return (unit * extent * 0.99).astype(jnp.bfloat16)


def draw_latents(key, part):
    key = jax.random.fold_in(key, 5)
    values = jnp.clip(jax.random.normal(key, (LEVELS, D), jnp.float32), -6.0, 6.0)
    return values


def place_ends(values, key, smallest, high):
    place = [jax.random.randint(jax.random.fold_in(key, axis), (), 0, length) for axis, length in enumerate(values.shape)]
    longest = values.shape.index(max(values.shape))
    next_to = place[:longest] + [(place[longest] + 1) % values.shape[longest]] + place[longest + 1:]
    return values.at[tuple(place)].set(smallest).at[tuple(next_to)].set(high)


def steps_of(key, shape, pieces, smallest, top_value):
    def one(position, blocks):
        heights = jax.random.uniform(jax.random.fold_in(jax.random.fold_in(key, 6), position), (blocks,), jnp.float32, smallest / len(pieces), top_value / len(pieces))
        return jnp.repeat(jnp.exp(heights), shape[position] // blocks).reshape((-1,) + (1,) * (len(shape) - position - 1))

    level = one(*pieces[0])
    for cut in pieces[1:]:
        level = level * one(*cut)
    return level


def routed_block(rng, own, number, rows, count, top, limit, skew):
    order = jax.random.permutation(rng, count)
    heavy_load, usual = portions_of(count, rows * top, limit, skew, True), portions_of(count, rows * top, limit, skew, False)
    places = jnp.arange(count)

    def named(tallies, rotation):
        used = int((tallies > 0).sum())
        fixed = max(1, used // 4)
        shifted = fixed + (places - fixed + rotation * (used - fixed)) % max(1, count - fixed)
        return jnp.zeros((count,), jnp.int32).at[order[jnp.where(places < fixed, places, shifted)]].set(jnp.asarray(tallies, jnp.int32))

    tallies = jnp.where(number % 4 == 0, named(heavy_load, number // 4), named(usual, number - number // 4 - 1))
    mixed = jax.random.permutation(jax.random.fold_in(own, 3), count)
    source_of, sink = mixed[0:count // 2 * 2:2], mixed[1:count // 2 * 2:2]
    slack = jnp.minimum(tallies[source_of] - 1, limit - tallies[sink]) // 2
    slack = jnp.where((source_of == order[0]) | (sink == order[0]) | (tallies[sink] == 0), 0, jnp.maximum(slack, 0))
    shifted = jax.random.randint(jax.random.fold_in(own, 4), (count // 2,), 0, 1 << 20) % (slack + 1)
    tallies = tallies.at[source_of].add(-shifted).at[sink].add(shifted)
    members = jnp.searchsorted(jnp.cumsum(tallies), jnp.arange(rows * top), side="right").astype(jnp.int32)
    listing = members.reshape(top, rows).T
    listing = listing[jax.random.permutation(jax.random.fold_in(own, 1), rows)]
    rotation = jax.random.randint(jax.random.fold_in(own, 2), (rows, 1), 0, top)
    return jnp.take_along_axis(listing, (jnp.arange(top)[None, :] + rotation) % top, axis=1)


def portions_of(amount, total, bound, skew, full):
    portions = [(1 << 20) // math.isqrt(rank ** skew) + 1 for rank in range(1, amount + 1)]
    largest = bound if full else min(bound, max(-(-total // amount), total * portions[0] // sum(portions)))
    least = 1 if total - largest >= amount - 1 else 0
    given, rest = [largest] + [least] * (amount - 1), total - largest - least * (amount - 1)
    while rest > 0:
        candidates = [i for i in range(1, amount) if given[i] < largest] or [i for i in range(1, amount) if given[i] < bound]
        pool, left = sum([portions[i] for i in candidates]), rest
        for i in candidates:
            addition = min(bound - given[i], max(1, left * portions[i] // pool), rest)
            given[i] = given[i] + addition
            rest = rest - addition
    return np.array(given)


def normal_values(own_key, shape, deviation, limit, pieces=(), held_as=jnp.bfloat16):
    loudness = steps_of(own_key, shape, pieces, -0.22, 0.18) if pieces else 1.0
    values = jax.random.normal(own_key, shape, jnp.float32) * deviation * loudness
    return jnp.minimum(jnp.maximum(values, -limit), limit).astype(held_as)


def setup_inputs(seed: int = 0) -> dict:
    key_list = jax.random.split(jax.random.key(seed), 11)
    swath = normal_values(key_list[0], (SOURCES, TILES, CH, FP), 1.0, 6.0, ((0, 8), (1, 32)))
    tile_band_keys = jax.random.split(jax.random.fold_in(key_list[1], 1), SOURCES * TILES // TILE_DEV)
    tile_band_turns = jax.random.permutation(jax.random.fold_in(key_list[1], 3), SOURCES * TILES // TILE_DEV)
    tile_band = jax.vmap(lambda own, number: routed_block(jax.random.fold_in(key_list[1], 2), own, number, TILE_DEV, N_LAT, 1, CAP, 2))(tile_band_keys, tile_band_turns).reshape((SOURCES, TILES, 1))
    tile_patch = place_ends(jax.random.randint(key_list[2], (SOURCES, TILES), 0, PATCH_DEV), jax.random.fold_in(key_list[2], 1), 0, PATCH_DEV - 1).astype(jnp.int32)
    fp_pos = draw_fp_pos(jax.random.fold_in(key_list[10], 71), 0)
    conv_weight = normal_values(key_list[4], (SOURCES, KS, KS, CH, D), (KS * KS * CH) ** -0.5, 0.0625, ((0, 8), (4, 32)))
    conv_bias = normal_values(key_list[5], (SOURCES, D), 1.0, 6.0, ((0, 8),), jnp.float32)
    norm_gain = jnp.clip(1.0 + 0.18 * jax.random.normal(key_list[6], (D,), jnp.float32), 0.1, 1.9)
    latents = draw_latents(jax.random.fold_in(key_list[10], 71), 0)
    kv_weight = normal_values(key_list[8], (D, 2 * D), D ** -0.5, 0.25)
    out_weight = normal_values(key_list[9], (D, D), D ** -0.5, 0.25)
    return {"swath": swath, "tile_band": tile_band, "tile_patch": tile_patch, "fp_pos": fp_pos, "conv_weight": conv_weight, "conv_bias": conv_bias, "norm_gain": norm_gain, "latents": latents, "kv_weight": kv_weight, "out_weight": out_weight}


def kernel_table(positions):
    cell_index = jnp.arange(PH * PW, dtype=jnp.int32)
    row_center = (cell_index // PW).astype(jnp.float32) + 0.5
    col_center = (cell_index % PW).astype(jnp.float32) + 0.5
    rows_at = positions[..., 0, :].astype(jnp.float32)[..., None]
    cols_at = positions[..., 1, :].astype(jnp.float32)[..., None]
    distance = (rows_at - row_center) ** 2 + (cols_at - col_center) ** 2
    return jnp.exp(-distance / 1.125).astype(jnp.bfloat16)

def grid_source(inputs):
    tiles, positions, targets, weight, bias = inputs

    def step(state_pair, block_index):
        numer, dens = state_pair
        start_row = (block_index * TILE_DEV).astype(jnp.int32)
        tile_now = lax.dynamic_slice_in_dim(tiles, start_row, TILE_DEV, 0)
        pos_now = lax.dynamic_slice_in_dim(positions, start_row, TILE_DEV, 0)
        target_now = lax.dynamic_slice_in_dim(targets, start_row, TILE_DEV, 0)
        kernel_bf = kernel_table(pos_now)
        contrib = jnp.einsum('jcf,jfx->jcx', tile_now.astype(jnp.float32), kernel_bf.astype(jnp.float32))
        weight_mass = lax.optimization_barrier(jnp.sum(kernel_bf.astype(jnp.float32), axis=1))
        numer = numer + jax.ops.segment_sum(contrib, target_now, num_segments=PATCHES)
        dens = dens + jax.ops.segment_sum(weight_mass, target_now, num_segments=PATCHES)
        return ((numer, dens), 0)
    init_state = (jnp.zeros((PATCHES, CH, PH * PW), jnp.float32), jnp.zeros((PATCHES, PH * PW), jnp.float32))
    block_ids = jnp.arange(TILES // TILE_DEV, dtype=jnp.int32)
    (numer, dens), _ = lax.scan(step, init_state, block_ids)
    gridded = (numer / (dens + 1.0)[:, None, :]).astype(jnp.bfloat16)
    blocks_six = gridded.reshape(PATCHES, CH, PH // KS, KS, PW // KS, KS).astype(jnp.float32)
    conv_out = jnp.einsum('pcakbl,klcd->pabd', blocks_six, weight.astype(jnp.float32))
    return (conv_out.reshape(PATCHES, TPS, D) + bias[None, None, :]).astype(jnp.bfloat16)

def reference(swath, tile_band, tile_patch, fp_pos, conv_weight, conv_bias, norm_gain, latents, kv_weight, out_weight):
    targets = (tile_band[..., 0] * PATCH_DEV + tile_patch).astype(jnp.int32)
    tokens = lax.map(grid_source, (swath, fp_pos, targets, conv_weight, conv_bias))
    sequence = jnp.transpose(tokens, (1, 0, 2, 3)).reshape(PATCHES, SOURCES * TPS, D)
    float_seq = sequence.astype(jnp.float32)
    row_mean = lax.optimization_barrier(jnp.mean(float_seq, axis=-1, keepdims=True))
    row_var = lax.optimization_barrier(jnp.mean((float_seq - row_mean) ** 2, axis=-1, keepdims=True))
    normed = ((float_seq - row_mean) * lax.rsqrt(row_var + 1e-05) * norm_gain).astype(jnp.bfloat16)
    keys_values = jnp.dot(normed.reshape(-1, D), kv_weight, preferred_element_type=jnp.float32).astype(jnp.bfloat16)
    keys_values = keys_values.reshape(PATCHES, SOURCES * TPS, 2 * D)
    keys_heads = keys_values[..., :D].reshape(PATCHES, SOURCES * TPS, HEADS, HD).astype(jnp.float32)
    value_heads = keys_values[..., D:].reshape(PATCHES, SOURCES * TPS, HEADS, HD).astype(jnp.float32)
    queries = latents.reshape(LEVELS, HEADS, HD)
    scores = jnp.einsum('lhe,pthe->plht', queries, keys_heads) * (1.0 / math.sqrt(HD))
    top_score = lax.optimization_barrier(jnp.max(scores, axis=-1, keepdims=True))
    expo = jnp.exp(scores - top_score)
    probs = (expo / lax.optimization_barrier(jnp.sum(expo, axis=-1, keepdims=True))).astype(jnp.bfloat16)
    attended = jnp.einsum('plht,pthe->plhe', probs.astype(jnp.float32), value_heads).astype(jnp.bfloat16)
    attended = attended.reshape(PATCHES * LEVELS, D)
    return jnp.dot(attended, out_weight, preferred_element_type=jnp.float32).reshape(PATCHES, LEVELS, D)
```

```python
import functools
import math

import jax
import jax.numpy as jnp
import numpy as np
from jax import lax
from jax.experimental import pallas as pl
from jax.experimental.pallas import tpu as pltpu
from jax.sharding import PartitionSpec as P

HEADS = 8
HD = 64
PW = 24
KS = 4
TPS = 12
LEVELS = 4
TILES = 32
PATCHES = 32
CHIPS = 16
SIDE = 4
CELLS = 192
TAPS = KS * KS
SLOTS = 4
FP = 128
PAIR = 2 * TPS
FAR = 1.0e4
OFFSETS = (0, -1, 1, 2)
ROW_TOKEN = np.array(list(range(TPS)) + [8, 9, 10, 11, 0, 1, 2, 3, 4, 5, 6, 7])
BF = jnp.bfloat16
F32 = jnp.float32
NT = (((1,), (1,)), ((), ()))
VMEM_LIMIT = 56 * 2**20


def centers(tokens):
    rows, cols = [], []
    for tap in range(TAPS):
        for token in tokens:
            rows.append(token // 6 * KS + tap // KS + 0.5 if token >= 0 else FAR)
            cols.append(token % 6 * KS + tap % KS + 0.5 if token >= 0 else FAR)
    wide = [np.repeat(np.array(v, np.float32)[:, None], FP, 1) for v in (rows, cols)]
    return np.stack(wide)


def weights_at(pos, center_ref, index):
    down = pos[0:1] - center_ref[index]
    across = pos[1:2] - center_ref[index + 1]
    return jnp.exp((down * down + across * across) * (-1.0 / 1.125))


def mass_kernel(pos_ref, center_ref, out_ref):
    ones = jnp.ones((8, FP), BF)
    place = lax.broadcasted_iota(jnp.int32, (8, CELLS), 0)

    def group(g, carry):
        base = pl.multiple_of(g * 8, 8)
        total = jnp.zeros((8, CELLS), F32)
        for j in range(8):
            table = weights_at(pos_ref[base + j], center_ref, 0).astype(BF)
            row = lax.dot_general(ones, table, NT, preferred_element_type=F32)
            total = jnp.where(place == j, row, total)
        out_ref[pl.ds(base, 8), :] = total
        return carry

    lax.fori_loop(0, TILES // 8, group, 0)


def tile_mass(pos):
    return pl.pallas_call(
        mass_kernel,
        out_shape=jax.ShapeDtypeStruct((TILES, CELLS), F32),
        cost_estimate=pl.CostEstimate(flops=2 * TILES * 8 * FP * CELLS, bytes_accessed=300000, transcendentals=TILES * FP * CELLS),
        name="tile_mass",
    )(pos, jnp.asarray(centers(range(TPS))))


def grid_kernel(swath_ref, pos_ref, inverse_ref, center_ref, out_ref):
    blocks = []
    gap = jnp.zeros((TAPS, 8, FP), F32)
    channels = swath_ref.shape[1]
    for pair in range(2):
        first, second = 2 * pair, 2 * pair + 1
        left = weights_at(pos_ref[first], center_ref, 0).reshape(TAPS, 16, FP)
        right = weights_at(pos_ref[second], center_ref, 2).reshape(TAPS, 16, FP)
        left = jnp.concatenate([left, gap], 1).reshape(TAPS * PAIR, FP)
        right = jnp.concatenate([gap, right], 1).reshape(TAPS * PAIR, FP)
        table = jnp.concatenate([left, right], 1).astype(BF)
        data = jnp.concatenate([swath_ref[first], swath_ref[second]], 1)
        total = lax.dot_general(table, data, NT, preferred_element_type=F32)
        scale = jnp.broadcast_to(inverse_ref[pair], (FP, TAPS * PAIR)).T
        scale = jnp.concatenate([scale] * (-(-channels // FP)), 1)[:, :channels]
        blocks.append((total * scale).reshape(TAPS, PAIR, channels))
    out_ref[...] = jnp.concatenate(blocks, 1).astype(BF)


def gridded(swath, pos, inverse, center):
    channels = swath.shape[1]
    return pl.pallas_call(
        grid_kernel,
        grid=(TILES // 4,),
        in_specs=[
            pl.BlockSpec((4, channels, FP), lambda i: (i, 0, 0)),
            pl.BlockSpec((4, 2, FP), lambda i: (i, 0, 0)),
            pl.BlockSpec((2, 1, TAPS * PAIR), lambda i: (i, 0, 0)),
            pl.BlockSpec((4, TAPS * 16, FP), lambda i: (0, 0, 0)),
        ],
        out_specs=pl.BlockSpec((TAPS, 2 * PAIR, channels), lambda i: (0, i, 0)),
        out_shape=jax.ShapeDtypeStruct((TAPS, TILES * TPS, channels), BF),
        compiler_params=pltpu.CompilerParams(vmem_limit_bytes=VMEM_LIMIT),
        cost_estimate=pl.CostEstimate(
            flops=2 * (TILES // 2) * TAPS * PAIR * 2 * FP * 768,
            bytes_accessed=TILES * channels * (FP + CELLS) * 2,
            transcendentals=TILES * FP * 256,
        ),
        name="grid_tiles",
    )(swath, pos, inverse, center)


def embed_kernel(own_ref, sib_ref, w0, w1, w2, w3, w4, column_ref, row_ref, out_ref, total, spread):
    step = pl.program_id(0)
    slot_rows = out_ref.shape[0]
    part = slot_rows // TAPS

    @pl.when(step == 0)
    def _():
        total[...] = jnp.zeros_like(total)

    channels = own_ref.shape[2]
    weight = jnp.concatenate([w[...].reshape(-1, channels) for w in (w0, w1, w2, w3, w4)], 0)
    half = TILES * TPS
    total[:half] += lax.dot_general(own_ref[0], weight, NT, preferred_element_type=F32)
    total[half:] += lax.dot_general(sib_ref[0], weight, NT, preferred_element_type=F32)
    base = pl.multiple_of(step * part, part)
    here = lax.broadcasted_iota(jnp.int32, (part, 2 * half), 0) + base
    spread[pl.ds(base, part), :] = jnp.where(here == row_ref[...], 1.0, 0.0).astype(BF)

    @pl.when(step == TAPS - 1)
    def _():
        width = total.shape[1]
        columns = lax.broadcasted_iota(jnp.int32, (width, width), 0)
        order = jnp.where(columns == column_ref[...], 1.0, 0.0).astype(BF)
        tokens = total[...].astype(BF)
        tokens = lax.dot_general(tokens, order, NT, preferred_element_type=F32).astype(BF)
        out_ref[...] = jnp.dot(spread[...], tokens, preferred_element_type=F32).astype(BF)


def embed(own, sib, weights, columns, rows):
    channels = own.shape[2]
    cols = weights[0].shape[2]
    width = CHIPS * cols
    slot_rows = 32 * SLOTS * TPS
    half = TILES * TPS
    return pl.pallas_call(
        embed_kernel,
        grid=(TAPS,),
        in_specs=[pl.BlockSpec((1, half, channels), lambda i: (i, 0, 0))] * 2
        + [pl.BlockSpec((w.shape[0], 1, cols, channels), lambda i: (0, i, 0, 0)) for w in weights]
        + [
            pl.BlockSpec((1, width), lambda i: (0, 0)),
            pl.BlockSpec((1, 2 * half), lambda i: (0, 0)),
        ],
        out_specs=pl.BlockSpec((slot_rows, width), lambda i: (0, 0)),
        out_shape=jax.ShapeDtypeStruct((slot_rows, width), BF),
        scratch_shapes=[pltpu.VMEM((2 * half, width), F32), pltpu.VMEM((slot_rows, 2 * half), BF)],
        compiler_params=pltpu.CompilerParams(vmem_limit_bytes=VMEM_LIMIT),
        cost_estimate=pl.CostEstimate(
            flops=2 * TAPS * 2 * half * 768 * width,
            bytes_accessed=TAPS * (2 * half + width) * 640 * 2,
            transcendentals=0,
        ),
        name="embed_tiles",
    )(own, sib, *weights, columns, rows)


def attend_kernel(tokens_ref, row_ref, bias_ref, gain_ref, kv_ref, latent_ref, out_ref):
    rows = TPS * PATCHES
    per_core = tokens_ref.shape[0] * tokens_ref.shape[2]
    width = 2 * tokens_ref.shape[3]
    hot = lax.broadcasted_iota(jnp.int32, (rows, per_core), 0) == row_ref[...]
    hot = jnp.where(hot, 1.0, 0.0).astype(BF)
    halves = [
        jnp.dot(hot, tokens_ref[:, c].reshape(per_core, width // 2), preferred_element_type=F32) for c in range(2)
    ]
    tokens = (jnp.concatenate(halves, 1) + bias_ref[...]).astype(BF).astype(F32)
    mean = jnp.mean(tokens, axis=1, keepdims=True)
    shifted = tokens - mean
    var = jnp.mean(shifted * shifted, axis=1, keepdims=True)
    normed = (shifted * lax.rsqrt(var + 1e-05) * gain_ref[...]).astype(BF)
    keys_values = jnp.dot(normed, kv_ref[...], preferred_element_type=F32).astype(BF)
    keys, values = keys_values[:, :width], keys_values[:, width:].astype(F32)
    head = lax.broadcasted_iota(jnp.int32, (HEADS, width), 0)
    lane_head = lax.shift_right_logical(lax.broadcasted_iota(jnp.int32, (HEADS, width), 1), int(math.log2(HD)))
    query = jnp.concatenate(
        [jnp.where(head == lane_head, jnp.broadcast_to(latent_ref[l : l + 1], (HEADS, width)), 0.0) for l in range(LEVELS)],
        0,
    )
    scores = jnp.zeros((rows, LEVELS * HEADS), F32)
    for _ in range(3):
        piece = query.astype(BF)
        scores += lax.dot_general(keys, piece, NT, preferred_element_type=F32)
        query = query - piece.astype(F32)
    scores = (scores * (1.0 / math.sqrt(HD))).reshape(TPS, PATCHES, LEVELS * HEADS)
    top = jnp.max(scores, axis=0)
    expo = jnp.exp(scores - top[None])
    mass = jnp.sum(expo, axis=0)
    expo = expo.reshape(rows, LEVELS * HEADS).astype(BF)
    values = values.reshape(TPS, PATCHES, width)
    parts = []
    for value, count in ((top, 3), (mass, 2)):
        for _ in range(count):
            piece = value.astype(BF)
            parts.append(piece)
            value = value - piece.astype(F32)
    pick = lax.broadcasted_iota(jnp.int32, (LEVELS * HEADS, width), 0)
    stat_row = lax.broadcasted_iota(jnp.int32, (LEVELS * HEADS, FP), 0)
    stat_lane = lax.broadcasted_iota(jnp.int32, (LEVELS * HEADS, FP), 1)
    lane = lax.shift_right_logical(lax.broadcasted_iota(jnp.int32, (LEVELS * HEADS, width), 1), int(math.log2(HD)))
    blocks = []
    for level in range(LEVELS):
        wide = jnp.where(pick == lane + level * HEADS, 1.0, 0.0).astype(BF)
        share = jnp.dot(expo, wide, preferred_element_type=F32).reshape(TPS, PATCHES, width)
        partial = jnp.sum(share * values, axis=0)
        stats = jnp.zeros((PATCHES, FP), F32)
        for n, piece in enumerate(parts):
            to = (stat_row - level * HEADS == stat_lane - n * HEADS) & (stat_row >= level * HEADS) & (stat_row < (level + 1) * HEADS)
            stats += jnp.dot(piece, jnp.where(to, 1.0, 0.0).astype(BF), preferred_element_type=F32)
        blocks.append(jnp.concatenate([partial, stats], 1).astype(BF))
    stacked = jnp.concatenate(blocks, 0)
    count = LEVELS * PATCHES
    target = lax.broadcasted_iota(jnp.int32, (count, count), 0)
    source = lax.broadcasted_iota(jnp.int32, (count, count), 1)
    moved = (target & (LEVELS - 1)) * PATCHES + lax.shift_right_logical(target, 2) == source
    out_ref[...] = jnp.dot(jnp.where(moved, 1.0, 0.0).astype(BF), stacked, preferred_element_type=F32).astype(BF)


def attend(tokens, rows, bias, gain, kv_weight, latents):
    width = kv_weight.shape[0]
    return pl.pallas_call(
        attend_kernel,
        out_shape=jax.ShapeDtypeStruct((PATCHES * LEVELS, width + FP), BF),
        compiler_params=pltpu.CompilerParams(vmem_limit_bytes=VMEM_LIMIT),
        cost_estimate=pl.CostEstimate(flops=2 * 384 * 512 * 4000, bytes_accessed=3000000, transcendentals=12288),
        name="attend_source",
    )(tokens, rows, bias, gain, kv_weight, latents)


def finish_kernel(parts_ref, weight_ref, out_ref):
    sources, rows, wide = parts_ref.shape
    width = wide - FP
    stats = parts_ref[:, :, width:].reshape(sources * rows, FP)
    row = lax.broadcasted_iota(jnp.int32, (FP, width), 0)
    head = lax.shift_right_logical(lax.broadcasted_iota(jnp.int32, (FP, width), 1), int(math.log2(HD)))
    same = (row & (HEADS - 1)) == head
    is_top = jnp.where(same & (row < 3 * HEADS), 1.0, 0.0).astype(BF)
    is_mass = jnp.where(same & (row >= 3 * HEADS) & (row < 5 * HEADS), 1.0, 0.0).astype(BF)
    top = jnp.dot(stats, is_top, preferred_element_type=F32).reshape(sources, rows, width)
    mass = jnp.dot(stats, is_mass, preferred_element_type=F32).reshape(sources, rows, width)
    scale = jnp.exp(top - jnp.max(top, axis=0)[None])
    above = jnp.sum(scale * parts_ref[:, :, :width].astype(F32), axis=0)
    attended = (above / jnp.sum(scale * mass, axis=0)).astype(BF)
    out_ref[...] = jnp.dot(attended, weight_ref[...], preferred_element_type=F32)


def finish(parts, out_weight):
    return pl.pallas_call(
        finish_kernel,
        out_shape=jax.ShapeDtypeStruct((parts.shape[1], out_weight.shape[1]), F32),
        cost_estimate=pl.CostEstimate(flops=2 * 128 * 128 * 1024, bytes_accessed=800000, transcendentals=65536),
        name="combine_sources",
    )(parts, out_weight)


def device_at(y, x, core):
    return ((y % SIDE) * SIDE + x % SIDE) * 2 + core


def shift(offset, second):
    pairs = []
    for y in range(SIDE):
        for x in range(SIDE):
            for core in range(2):
                along_x = (core == 0) != second
                to = device_at(y, x + offset, core) if along_x else device_at(y + offset, x, core)
                pairs.append((device_at(y, x, core), to))
    return pairs


def send(array, offset, second):
    return lax.ppermute(array, "lat", shift(offset, second))


def gather_weights(shard):
    half = TAPS // 2
    up, down = send(shard, 1, False), send(shard, -1, False)
    far = [send(up[:half], 1, False), send(down[half:], -1, False)]
    line = jnp.stack([shard, up, down, jnp.concatenate(far, 0)], 0)
    above, below = send(line, 1, True), send(line, -1, True)
    return [line, above, below, send(above[:2], 1, True), send(below[2:], -1, True)]


def body(
    swath,
    tile_band,
    tile_patch,
    fp_pos,
    conv_weight,
    conv_bias,
    norm_gain,
    latents,
    kv_weight,
    out_weight,
):
    place = lax.axis_index("lat")
    core, chip = place % 2, place // 2
    chip_y, chip_x = chip // SIDE, chip % SIDE
    swath, fp_pos = swath[0], fp_pos[0]
    channels, cols = swath.shape[1], conv_weight.shape[4]
    width = kv_weight.shape[0]
    swap = [(i, i ^ 1) for i in range(2 * CHIPS)]

    shard = jnp.transpose(conv_weight[0].reshape(TAPS, channels, cols), (0, 2, 1))
    weights = gather_weights(shard)
    sib_swath = lax.ppermute(swath, "lat", swap)
    pos = fp_pos.astype(F32)
    sib_pos = lax.ppermute(fp_pos, "lat", swap).astype(F32)

    about = jnp.stack([tile_band[0, :, 0], tile_patch[0]], 1).astype(F32)
    record = jnp.concatenate([tile_mass(pos), about, jnp.zeros((TILES, 256 - CELLS - 2), F32)], 1)
    records = lax.all_gather(record, "lat")
    bands = records[:, :, CELLS].astype(jnp.int32)
    patches = records[:, :, CELLS + 1].astype(jnp.int32)
    target = bands * PATCHES + patches
    earlier = jnp.asarray(np.tril(np.ones((TILES, TILES), np.int32), -1))
    rank = jnp.sum((bands[:, :, None] == bands[:, None, :]).astype(jnp.int32) * earlier, axis=2)

    pick = jnp.stack([place, place ^ 1])
    bands_here, rank_here = jnp.take(bands, pick, axis=0), jnp.take(rank, pick, axis=0)
    target_here = jnp.take(target, pick, axis=0).reshape(2 * TILES)
    same = (target_here[:, None] == target.reshape(-1)[None, :]).astype(F32)
    density = 1.0 + jnp.dot(
        same, records[:, :, :CELLS].reshape(-1, CELLS), precision=lax.Precision.HIGHEST, preferred_element_type=F32
    )
    inverse = (1.0 / density).reshape(TILES, 2, TAPS, TPS)
    even, odd = inverse[:, 0], inverse[:, 1]
    inverse = jnp.concatenate([even, odd[..., 8:], odd[..., :8]], -1).reshape(2, TILES // 2, 1, TAPS * PAIR)

    center = jnp.asarray(
        np.concatenate([centers(list(range(TPS)) + [-1] * 4), centers([-1] * 4 + list(ROW_TOKEN[TPS:]))], 0)
    )
    own = gridded(swath, pos, inverse[0], center)
    sib = gridded(sib_swath, sib_pos, inverse[1], center)

    origin = jnp.stack([core, 1 - core])[:, None]
    slot = (bands_here * SLOTS + 2 * origin + rank_here) * TPS
    token_rows = jnp.asarray(np.tile(ROW_TOKEN, TILES))
    rows = (jnp.repeat(slot.reshape(-1), TPS) + token_rows)[None, :].astype(jnp.int32)
    near = jnp.tile(jnp.asarray(OFFSETS), SIDE)
    farther = jnp.repeat(jnp.asarray(OFFSETS), SIDE)
    at_y = (chip_y + jnp.where(core == 0, farther, near)) % SIDE
    at_x = (chip_x + jnp.where(core == 0, near, farther)) % SIDE
    columns = (jnp.repeat((at_y * SIDE + at_x) * cols, cols) + jnp.asarray(np.tile(np.arange(cols), CHIPS)))[None, :]
    outgoing = embed(own, sib, weights, columns.astype(jnp.int32), rows)

    outgoing = outgoing.reshape(2 * CHIPS, SLOTS * TPS, CHIPS * cols)
    incoming = lax.all_to_all(outgoing, "lat", split_axis=0, concat_axis=0, tiled=True)
    mine = (bands == place)[:, :, None] & (rank[:, :, None] == jnp.arange(2)[None, None, :])
    patch_in = jnp.sum(jnp.where(mine, patches[:, :, None] + 1, 0), axis=1).reshape(-1, 1) - 1
    token_in = jnp.where(patch_in < 0, -1, patch_in + PATCHES * jnp.arange(TPS)[None, :]).reshape(1, -1)

    def by_core(array):
        shape = array.shape[1:]
        split = array.reshape((CHIPS, 2, cols) + shape)
        return jnp.swapaxes(split, 0, 1).reshape((width,) + shape)

    parts = attend(
        incoming.reshape(CHIPS, 2, SLOTS * TPS, CHIPS * cols),
        token_in.astype(jnp.int32),
        by_core(conv_bias[0])[None],
        by_core(norm_gain)[None],
        by_core(kv_weight),
        latents,
    )
    sources = lax.axis_size("src")
    parts = lax.all_to_all(
        parts.reshape(sources, -1, width + FP), "src", split_axis=0, concat_axis=0, tiled=True
    )
    return finish(parts, out_weight).reshape(-1, LEVELS, width)


def solution(mesh):
    in_specs = (
        P("src", "lat", None, None),
        P("src", "lat", None),
        P("src", "lat"),
        P("src", "lat", None, None),
        P("src", None, None, None, "lat"),
        P("src", None),
        P(),
        P(),
        P(),
        P(),
    )
    out_specs = P(("lat", "src"), None, None)
    return jax.shard_map(body, mesh=mesh, in_specs=in_specs, out_specs=out_specs, check_vma=False)
```

```python
import math

import jax
import jax.numpy as jnp
import numpy as np
from jax import lax
from jax.experimental import pallas as pl
from jax.experimental.pallas import tpu as pltpu
from jax.sharding import PartitionSpec as P

HEADS = 8
HD = 64
PW = 24
KS = 4
TPS = 12
LEVELS = 4
TILES = 32
PATCHES = 32
CHIPS = 16
SIDE = 4
CELLS = 192
TAPS = KS * KS
SLOTS = 4
FP = 128
PAIR = 2 * TPS
FAR = 1.0e4
OFFSETS = (0, -1, 1, 2)
ROW_TOKEN = np.array(list(range(TPS)) + [8, 9, 10, 11, 0, 1, 2, 3, 4, 5, 6, 7])
BF = jnp.bfloat16
F32 = jnp.float32
NT = (((1,), (1,)), ((), ()))
KERNEL_VMEM = 24 * 2**20
RECORD = 256


def centers(tokens):
    rows, cols = [], []
    for tap in range(TAPS):
        for token in tokens:
            rows.append(token // 6 * KS + tap // KS + 0.5 if token >= 0 else FAR)
            cols.append(token % 6 * KS + tap % KS + 0.5 if token >= 0 else FAR)
    wide = [np.repeat(np.array(v, np.float32)[:, None], FP, 1) for v in (rows, cols)]
    return np.stack(wide)


def weights_at(pos, center_ref, index):
    down = pos[0:1] - center_ref[index]
    across = pos[1:2] - center_ref[index + 1]
    return jnp.exp((down * down + across * across) * (-1.0 / 1.125))


def mass_kernel(pos_ref, center_ref, out_ref):
    ones = jnp.ones((8, FP), BF)
    place = lax.broadcasted_iota(jnp.int32, (8, CELLS), 0)

    def group(g, carry):
        base = pl.multiple_of(g * 8, 8)
        total = jnp.zeros((8, CELLS), F32)
        for j in range(8):
            table = weights_at(pos_ref[base + j].astype(F32), center_ref, 0).astype(BF)
            row = lax.dot_general(ones, table, NT, preferred_element_type=F32)
            total = jnp.where(place == j, row, total)
        target = jnp.broadcast_to(pos_ref[pl.ds(base, 8), 2].astype(F32) * PATCHES + pos_ref[pl.ds(base, 8), 3].astype(F32), (8, FP))
        out_ref[pl.ds(base, 8), :] = jnp.concatenate([total, target[:, : RECORD - CELLS]], 1)
        return carry

    lax.fori_loop(0, TILES // 8, group, 0)


def tile_records(pos):
    return pl.pallas_call(
        mass_kernel,
        out_shape=jax.ShapeDtypeStruct((TILES, RECORD), F32),
        cost_estimate=pl.CostEstimate(flops=2 * TILES * 8 * FP * CELLS, bytes_accessed=300000, transcendentals=TILES * FP * CELLS),
        name="tile_records",
    )(pos, jnp.asarray(centers(range(TPS))))


def inverse_kernel(record_ref, target_ref, row_tile_ref, own_cell_ref, tap_ref, out_ref):
    same = jnp.where(record_ref[:, CELLS : CELLS + 1] == target_ref[...], 1.0, 0.0).astype(BF)
    mass = record_ref[:, :CELLS]
    total = jnp.ones((CELLS, target_ref.shape[1]), F32)
    for _ in range(3):
        piece = mass.astype(BF)
        total += lax.dot_general(piece, same, (((0,), (0,)), ((), ())), preferred_element_type=F32)
        mass = mass - piece.astype(F32)
    inverse = 1.0 / total
    out = jnp.zeros(out_ref.shape, F32)
    for _ in range(3):
        piece = inverse.astype(BF)
        spread = jnp.dot(piece, row_tile_ref[...], preferred_element_type=F32).astype(BF) * own_cell_ref[...]
        out += jnp.dot(tap_ref[...], spread, preferred_element_type=F32)
        inverse = inverse - piece.astype(F32)
    out_ref[...] = out


def inverse_density(records, targets):
    rows = 2 * TILES * TPS
    row_tile = (np.arange(2 * TILES)[:, None] == np.arange(rows)[None, :] // TPS).astype(np.float32)
    token = np.tile(ROW_TOKEN, TILES)
    own_cell = (np.arange(CELLS)[:, None] % TPS == token[None, :]).astype(np.float32)
    tap = (np.arange(TAPS)[:, None] == np.arange(CELLS)[None, :] // TPS).astype(np.float32)
    return pl.pallas_call(
        inverse_kernel,
        out_shape=jax.ShapeDtypeStruct((TAPS, rows), F32),
        compiler_params=pltpu.CompilerParams(vmem_limit_bytes=KERNEL_VMEM),
        cost_estimate=pl.CostEstimate(flops=6 * 1024 * CELLS * 128, bytes_accessed=2000000, transcendentals=0),
        name="inverse_density",
    )(records, targets, *(jnp.asarray(v, BF) for v in (row_tile, own_cell, tap)))


def grid_kernel(swath_ref, pos_ref, center_ref, out_ref):
    channels = swath_ref.shape[1]
    gap = jnp.zeros((TAPS, 8, FP), F32)

    def step(tiles_ref):
        i = pl.program_id(0)
        blocks = []
        for pair in range(2):
            first, second = 4 * i + 2 * pair, 4 * i + 2 * pair + 1
            left = weights_at(pos_ref[first].astype(F32), center_ref, 0).reshape(TAPS, 16, FP)
            right = weights_at(pos_ref[second].astype(F32), center_ref, 2).reshape(TAPS, 16, FP)
            left = jnp.concatenate([left, gap], 1).reshape(TAPS * PAIR, FP)
            right = jnp.concatenate([gap, right], 1).reshape(TAPS * PAIR, FP)
            table = jnp.concatenate([left, right], 1).astype(BF)
            data = jnp.concatenate([tiles_ref[2 * pair], tiles_ref[2 * pair + 1]], 1)
            total = lax.dot_general(table, data, NT, preferred_element_type=F32)
            blocks.append(total.reshape(TAPS, PAIR, channels))
        base = pl.multiple_of(i * 2 * PAIR, 2 * PAIR)
        out_ref[:, pl.ds(base, 2 * PAIR), :] = jnp.concatenate(blocks, 1).astype(BF)

    pltpu.emit_pipeline(
        step, grid=(TILES // 4,), in_specs=[pl.BlockSpec((4, channels, FP), lambda i: (i, 0, 0))]
    )(swath_ref)


def gridded(swath, pos, center):
    channels = swath.shape[1]
    vmem = pl.BlockSpec(memory_space=pltpu.VMEM)
    return pl.pallas_call(
        grid_kernel,
        in_specs=[pl.BlockSpec(memory_space=pl.ANY), vmem, vmem],
        out_specs=vmem,
        out_shape=pltpu.VMEM((TAPS, TILES * TPS, channels), BF),
        compiler_params=pltpu.CompilerParams(vmem_limit_bytes=KERNEL_VMEM),
        cost_estimate=pl.CostEstimate(
            flops=2 * (TILES // 2) * TAPS * PAIR * 2 * FP * 768,
            bytes_accessed=TILES * channels * FP * 2,
            transcendentals=TILES * FP * 256,
        ),
        name="grid_tiles",
    )(swath, pos, center)


def embed_kernel(own_ref, sib_ref, w0, w1, w2, w3, w4, inverse_ref, column_ref, row_ref, out_ref, total, spread):
    channels = own_ref.shape[2]
    slot_rows, half = out_ref.shape[0], own_ref.shape[1]
    part = slot_rows // TAPS
    width = total.shape[1]
    total[...] = jnp.zeros_like(total)

    def tap(k, carry):
        weight = jnp.concatenate([w[:, k].reshape(-1, channels) for w in (w0, w1, w2, w3, w4)], 0)
        scale = jnp.broadcast_to(inverse_ref[pl.ds(k, 1), :], (FP, 2 * half)).T
        scale = jnp.concatenate([scale] * (width // FP), 1)
        for n, ref in enumerate((own_ref, sib_ref)):
            rows = slice(n * half, (n + 1) * half)
            product = lax.dot_general(ref[k], weight, NT, preferred_element_type=F32)
            total[rows] += product * scale[rows]
        base = pl.multiple_of(k * part, part)
        here = lax.broadcasted_iota(jnp.int32, (part, 2 * half), 0) + base
        spread[pl.ds(base, part), :] = jnp.where(here == row_ref[...], 1.0, 0.0).astype(BF)
        return carry

    lax.fori_loop(0, TAPS, tap, 0)
    columns = lax.broadcasted_iota(jnp.int32, (width, width), 0)
    order = jnp.where(columns == column_ref[...], 1.0, 0.0).astype(BF)
    tokens = lax.dot_general(total[...].astype(BF), order, NT, preferred_element_type=F32).astype(BF)
    out_ref[...] = jnp.dot(spread[...], tokens, preferred_element_type=F32).astype(BF)


def embed(own, sib, weights, inverse, columns, rows):
    width = CHIPS * weights[0].shape[2]
    slot_rows = 2 * CHIPS * SLOTS * TPS
    half = TILES * TPS
    vmem = pl.BlockSpec(memory_space=pltpu.VMEM)
    large = [pltpu.with_memory_space_constraint(a, pltpu.VMEM) for a in (own, sib, *weights)]
    return pl.pallas_call(
        embed_kernel,
        in_specs=[vmem] * (len(large) + 3),
        out_specs=vmem,
        out_shape=jax.ShapeDtypeStruct((slot_rows, width), BF),
        scratch_shapes=[pltpu.VMEM((2 * half, width), F32), pltpu.VMEM((slot_rows, 2 * half), BF)],
        compiler_params=pltpu.CompilerParams(vmem_limit_bytes=KERNEL_VMEM),
        cost_estimate=pl.CostEstimate(flops=2 * TAPS * 2 * half * 768 * width * 2, bytes_accessed=1000000, transcendentals=0),
        name="embed_tiles",
    )(*large, inverse, columns, rows)


def attend_kernel(tokens_ref, row_ref, bias_ref, gain_ref, kv_ref, latent_ref, out_ref):
    rows = TPS * PATCHES
    per_core = tokens_ref.shape[0] * tokens_ref.shape[2]
    width = 2 * tokens_ref.shape[3]
    hot = lax.broadcasted_iota(jnp.int32, (rows, per_core), 0) == row_ref[...]
    hot = jnp.where(hot, 1.0, 0.0).astype(BF)
    halves = [
        jnp.dot(hot, tokens_ref[:, c].reshape(per_core, width // 2), preferred_element_type=F32) for c in range(2)
    ]
    tokens = (jnp.concatenate(halves, 1) + bias_ref[...]).astype(BF).astype(F32)
    mean = jnp.mean(tokens, axis=1, keepdims=True)
    shifted = tokens - mean
    var = jnp.mean(shifted * shifted, axis=1, keepdims=True)
    normed = (shifted * lax.rsqrt(var + 1e-05) * gain_ref[...]).astype(BF)
    keys_values = jnp.dot(normed, kv_ref[...], preferred_element_type=F32).astype(BF)
    keys, values = keys_values[:, :width], keys_values[:, width:].astype(F32)
    head = lax.broadcasted_iota(jnp.int32, (HEADS, width), 0)
    lane_head = lax.shift_right_logical(lax.broadcasted_iota(jnp.int32, (HEADS, width), 1), int(math.log2(HD)))
    query = jnp.concatenate(
        [jnp.where(head == lane_head, jnp.broadcast_to(latent_ref[l : l + 1], (HEADS, width)), 0.0) for l in range(LEVELS)],
        0,
    )
    scores = jnp.zeros((rows, LEVELS * HEADS), F32)
    for _ in range(3):
        piece = query.astype(BF)
        scores += lax.dot_general(keys, piece, NT, preferred_element_type=F32)
        query = query - piece.astype(F32)
    scores = (scores * (1.0 / math.sqrt(HD))).reshape(TPS, PATCHES, LEVELS * HEADS)
    top = jnp.max(scores, axis=0)
    expo = jnp.exp(scores - top[None])
    mass = jnp.sum(expo, axis=0)
    expo = expo.reshape(rows, LEVELS * HEADS).astype(BF)
    values = values.reshape(TPS, PATCHES, width)
    parts = []
    for value, count in ((top, 3), (mass, 2)):
        for _ in range(count):
            piece = value.astype(BF)
            parts.append(piece)
            value = value - piece.astype(F32)
    pick = lax.broadcasted_iota(jnp.int32, (LEVELS * HEADS, width), 0)
    stat_row = lax.broadcasted_iota(jnp.int32, (LEVELS * HEADS, FP), 0)
    stat_lane = lax.broadcasted_iota(jnp.int32, (LEVELS * HEADS, FP), 1)
    lane = lax.shift_right_logical(lax.broadcasted_iota(jnp.int32, (LEVELS * HEADS, width), 1), int(math.log2(HD)))
    blocks = []
    for level in range(LEVELS):
        wide = jnp.where(pick == lane + level * HEADS, 1.0, 0.0).astype(BF)
        share = jnp.dot(expo, wide, preferred_element_type=F32).reshape(TPS, PATCHES, width)
        partial = jnp.sum(share * values, axis=0)
        stats = jnp.zeros((PATCHES, FP), F32)
        for n, piece in enumerate(parts):
            to = (stat_row - level * HEADS == stat_lane - n * HEADS) & (stat_row >= level * HEADS) & (stat_row < (level + 1) * HEADS)
            stats += jnp.dot(piece, jnp.where(to, 1.0, 0.0).astype(BF), preferred_element_type=F32)
        blocks.append(jnp.concatenate([partial, stats], 1).astype(BF))
    stacked = jnp.concatenate(blocks, 0)
    count = LEVELS * PATCHES
    target = lax.broadcasted_iota(jnp.int32, (count, count), 0)
    source = lax.broadcasted_iota(jnp.int32, (count, count), 1)
    moved = (target & (LEVELS - 1)) * PATCHES + lax.shift_right_logical(target, 2) == source
    out_ref[...] = jnp.dot(jnp.where(moved, 1.0, 0.0).astype(BF), stacked, preferred_element_type=F32).astype(BF)


def attend(tokens, rows, bias, gain, kv_weight, latents):
    width = kv_weight.shape[0]
    return pl.pallas_call(
        attend_kernel,
        out_shape=jax.ShapeDtypeStruct((PATCHES * LEVELS, width + FP), BF),
        compiler_params=pltpu.CompilerParams(vmem_limit_bytes=KERNEL_VMEM),
        cost_estimate=pl.CostEstimate(flops=2 * 384 * 512 * 4000, bytes_accessed=3000000, transcendentals=12288),
        name="attend_source",
    )(tokens, rows, bias, gain, kv_weight, latents)


def finish_kernel(parts_ref, weight_ref, out_ref):
    sources, rows, wide = parts_ref.shape
    width = wide - FP
    stats = parts_ref[:, :, width:].reshape(sources * rows, FP)
    row = lax.broadcasted_iota(jnp.int32, (FP, width), 0)
    head = lax.shift_right_logical(lax.broadcasted_iota(jnp.int32, (FP, width), 1), int(math.log2(HD)))
    same = (row & (HEADS - 1)) == head
    is_top = jnp.where(same & (row < 3 * HEADS), 1.0, 0.0).astype(BF)
    is_mass = jnp.where(same & (row >= 3 * HEADS) & (row < 5 * HEADS), 1.0, 0.0).astype(BF)
    top = jnp.dot(stats, is_top, preferred_element_type=F32).reshape(sources, rows, width)
    mass = jnp.dot(stats, is_mass, preferred_element_type=F32).reshape(sources, rows, width)
    scale = jnp.exp(top - jnp.max(top, axis=0)[None])
    above = jnp.sum(scale * parts_ref[:, :, :width].astype(F32), axis=0)
    attended = (above / jnp.sum(scale * mass, axis=0)).astype(BF)
    result = jnp.dot(attended, weight_ref[...], preferred_element_type=F32)
    for patch in range(rows // LEVELS):
        out_ref[patch] = result[patch * LEVELS : (patch + 1) * LEVELS]


def finish(parts, out_weight):
    return pl.pallas_call(
        finish_kernel,
        out_shape=jax.ShapeDtypeStruct((parts.shape[1] // LEVELS, LEVELS, out_weight.shape[1]), F32),
        cost_estimate=pl.CostEstimate(flops=2 * 128 * 128 * 1024, bytes_accessed=800000, transcendentals=65536),
        name="combine_sources",
    )(parts, out_weight)


def device_at(y, x, core):
    return ((y % SIDE) * SIDE + x % SIDE) * 2 + core


def shift(offset, second):
    pairs = []
    for y in range(SIDE):
        for x in range(SIDE):
            for core in range(2):
                along_x = (core == 0) != second
                to = device_at(y, x + offset, core) if along_x else device_at(y + offset, x, core)
                pairs.append((device_at(y, x, core), to))
    return pairs


def send(array, offset, second):
    return lax.ppermute(array, "lat", shift(offset, second))


def gather_weights(shard):
    half = TAPS // 2
    up, down = send(shard, 1, False), send(shard, -1, False)
    far = [send(up[:half], 1, False), send(down[half:], -1, False)]
    line = jnp.stack([shard, up, down, jnp.concatenate(far, 0)], 0)
    above, below = send(line, 1, True), send(line, -1, True)
    return [line, above, below, send(above[:2], 1, True), send(below[2:], -1, True)]


def body(
    swath,
    tile_band,
    tile_patch,
    fp_pos,
    conv_weight,
    conv_bias,
    norm_gain,
    latents,
    kv_weight,
    out_weight,
):
    place = lax.axis_index("lat")
    core, chip = place % 2, place // 2
    chip_y, chip_x = chip // SIDE, chip % SIDE
    swath, fp_pos = swath[0], fp_pos[0]
    channels, cols = swath.shape[1], conv_weight.shape[4]
    width = kv_weight.shape[0]
    swap = [(i, i ^ 1) for i in range(2 * CHIPS)]

    shard = jnp.transpose(conv_weight[0].reshape(TAPS, channels, cols), (0, 2, 1))
    weights = gather_weights(shard)
    sib_swath = lax.ppermute(swath, "lat", swap)
    band, patch = tile_band[0, :, 0], tile_patch[0]
    about = jnp.broadcast_to(jnp.stack([band, patch], 1).astype(BF)[:, :, None], fp_pos.shape)
    pos = jnp.concatenate([fp_pos, about], 1)
    sib_pos = lax.ppermute(pos, "lat", swap)

    records = lax.all_gather(tile_records(pos), "lat")
    center = jnp.asarray(
        np.concatenate([centers(list(range(TPS)) + [-1] * 4), centers([-1] * 4 + list(ROW_TOKEN[TPS:]))], 0)
    )
    own = gridded(swath, pos, center)
    sib = gridded(sib_swath, sib_pos, center)
    sib_about = sib_pos[:, 2:, 0].astype(jnp.int32)
    bands_here = jnp.stack([band, sib_about[:, 0]])
    patches_here = jnp.stack([patch, sib_about[:, 1]])
    targets = (bands_here * PATCHES + patches_here).reshape(1, -1).astype(F32)
    inverse = inverse_density(records.reshape(-1, RECORD), targets)

    earlier = jnp.asarray(np.tril(np.ones((TILES, TILES), np.int32), -1))

    def rank_of(named):
        return jnp.sum((named[:, :, None] == named[:, None, :]).astype(jnp.int32) * earlier, axis=2)

    origin = jnp.stack([core, 1 - core])[:, None]
    slot = (bands_here * SLOTS + 2 * origin + rank_of(bands_here)) * TPS
    token_rows = jnp.asarray(np.tile(ROW_TOKEN, TILES))
    rows = (jnp.repeat(slot.reshape(-1), TPS) + token_rows)[None, :].astype(jnp.int32)
    near = jnp.tile(jnp.asarray(OFFSETS), SIDE)
    farther = jnp.repeat(jnp.asarray(OFFSETS), SIDE)
    at_y = (chip_y + jnp.where(core == 0, farther, near)) % SIDE
    at_x = (chip_x + jnp.where(core == 0, near, farther)) % SIDE
    columns = (jnp.repeat((at_y * SIDE + at_x) * cols, cols) + jnp.asarray(np.tile(np.arange(cols), CHIPS)))[None, :]
    outgoing = embed(own, sib, weights, inverse, columns.astype(jnp.int32), rows)

    outgoing = outgoing.reshape(2 * CHIPS, SLOTS * TPS, CHIPS * cols)
    incoming = lax.all_to_all(outgoing, "lat", split_axis=0, concat_axis=0, tiled=True)
    target = records[:, :, CELLS].astype(jnp.int32)
    bands, patches = target // PATCHES, target % PATCHES
    rank = rank_of(bands)
    mine = (bands == place)[:, :, None] & (rank[:, :, None] == jnp.arange(2)[None, None, :])
    patch_in = jnp.sum(jnp.where(mine, patches[:, :, None] + 1, 0), axis=1).reshape(-1, 1) - 1
    token_in = jnp.where(patch_in < 0, -1, patch_in + PATCHES * jnp.arange(TPS)[None, :]).reshape(1, -1)

    def by_core(array):
        shape = array.shape[1:]
        split = array.reshape((CHIPS, 2, cols) + shape)
        return jnp.swapaxes(split, 0, 1).reshape((width,) + shape)

    parts = attend(
        incoming.reshape(CHIPS, 2, SLOTS * TPS, CHIPS * cols),
        token_in.astype(jnp.int32),
        by_core(conv_bias[0])[None],
        by_core(norm_gain)[None],
        by_core(kv_weight),
        latents,
    )
    sources = lax.axis_size("src")
    parts = lax.all_to_all(
        parts.reshape(sources, -1, width + FP), "src", split_axis=0, concat_axis=0, tiled=True
    )
    return finish(parts, out_weight)


def solution(mesh):
    in_specs = (
        P("src", "lat", None, None),
        P("src", "lat", None),
        P("src", "lat"),
        P("src", "lat", None, None),
        P("src", None, None, None, "lat"),
        P("src", None),
        P(),
        P(),
        P(),
        P(),
    )
    out_specs = P(("lat", "src"), None, None)
    return jax.shard_map(body, mesh=mesh, in_specs=in_specs, out_specs=out_specs, check_vma=False)
```

```python
import math

import jax
import jax.numpy as jnp
import numpy as np
from jax import lax
from jax.experimental import pallas as pl
from jax.experimental.pallas import tpu as pltpu
from jax.sharding import PartitionSpec as P

HEADS = 8
HD = 64
PW = 24
KS = 4
TPS = 12
LEVELS = 4
TILES = 32
PATCHES = 32
CHIPS = 16
SIDE = 4
CELLS = 192
TAPS = KS * KS
SLOTS = 4
FP = 128
PAIR = 2 * TPS
FAR = 1.0e4
OFFSETS = (0, -1, 1, 2)
ROW_TOKEN = np.array(list(range(TPS)) + [8, 9, 10, 11, 0, 1, 2, 3, 4, 5, 6, 7])
BF = jnp.bfloat16
F32 = jnp.float32
NT = (((1,), (1,)), ((), ()))
KERNEL_VMEM = 24 * 2**20
RECORD = 256


def centers(tokens):
    rows, cols = [], []
    for tap in range(TAPS):
        for token in tokens:
            rows.append(token // 6 * KS + tap // KS + 0.5 if token >= 0 else FAR)
            cols.append(token % 6 * KS + tap % KS + 0.5 if token >= 0 else FAR)
    wide = [np.repeat(np.array(v, np.float32)[:, None], FP, 1) for v in (rows, cols)]
    return np.stack(wide)


def weights_at(pos, center_ref, index):
    down = pos[0:1] - center_ref[index]
    across = pos[1:2] - center_ref[index + 1]
    return jnp.exp((down * down + across * across) * (-1.0 / 1.125))


def record_kernel(band_ref, patch_ref, pos_ref, center_ref, out_ref):
    ones = jnp.ones((8, FP), BF)
    place = lax.broadcasted_iota(jnp.int32, (8, RECORD), 0)
    lane = lax.broadcasted_iota(jnp.int32, (8, RECORD - CELLS), 1)

    def group(g, carry):
        base = pl.multiple_of(g * 8, 8)
        total = jnp.zeros((8, RECORD), F32)
        for j in range(8):
            table = weights_at(pos_ref[base + j].astype(F32), center_ref, 0).astype(BF)
            row = lax.dot_general(ones, table, NT, preferred_element_type=F32)
            about = jnp.where(lane == 0, band_ref[base + j], patch_ref[base + j]).astype(F32)
            total = jnp.where(place == j, jnp.concatenate([row, about], 1), total)
        return carry + (total,)

    rows = ()
    for g in range(TILES // 8):
        rows = group(g, rows)
    out_ref[...] = jnp.concatenate(rows, 0).astype(BF)


def tile_records(band, patch, pos):
    vmem, smem = pl.BlockSpec(memory_space=pltpu.VMEM), pl.BlockSpec(memory_space=pltpu.SMEM)
    return pl.pallas_call(
        record_kernel,
        in_specs=[smem, smem, vmem, vmem],
        out_shape=jax.ShapeDtypeStruct((TILES, RECORD), BF),
        cost_estimate=pl.CostEstimate(flops=2 * TILES * 8 * FP * CELLS, bytes_accessed=300000, transcendentals=TILES * FP * CELLS),
        name="tile_records",
    )(band, patch, pos, jnp.asarray(centers(range(TPS))))


def inverse_kernel(record_ref, target_ref, slot_ref, token_ref, row_tile_ref, own_cell_ref, tap_ref, out_ref, row_ref):
    about = record_ref[:, CELLS:].astype(F32)
    same = jnp.where(about[:, :1] * PATCHES + about[:, 1:2] == target_ref[...], 1.0, 0.0).astype(BF)
    total = lax.dot_general(record_ref[:, :CELLS], same, (((0,), (0,)), ((), ())), preferred_element_type=F32)
    inverse = 1.0 / (1.0 + total)
    out = jnp.zeros(out_ref.shape, F32)
    for _ in range(3):
        piece = inverse.astype(BF)
        spread = jnp.dot(piece, row_tile_ref[...], preferred_element_type=F32).astype(BF) * own_cell_ref[...]
        out += jnp.dot(tap_ref[...], spread, preferred_element_type=F32)
        inverse = inverse - piece.astype(F32)
    out_ref[...] = out
    slots = jnp.dot(jnp.broadcast_to(slot_ref[...], (8, slot_ref.shape[1])).astype(BF), row_tile_ref[...], preferred_element_type=F32)
    row_ref[...] = slots[:1].astype(jnp.int32) * TPS + token_ref[...]


def inverse_density(records, targets, slots):
    rows = 2 * TILES * TPS
    row_tile = (np.arange(2 * TILES)[:, None] == np.arange(rows)[None, :] // TPS).astype(np.float32)
    token = np.tile(ROW_TOKEN, TILES)
    own_cell = (np.arange(CELLS)[:, None] % TPS == token[None, :]).astype(np.float32)
    tap = (np.arange(TAPS)[:, None] == np.arange(CELLS)[None, :] // TPS).astype(np.float32)
    return pl.pallas_call(
        inverse_kernel,
        out_shape=(jax.ShapeDtypeStruct((TAPS, rows), F32), jax.ShapeDtypeStruct((1, rows), jnp.int32)),
        compiler_params=pltpu.CompilerParams(vmem_limit_bytes=KERNEL_VMEM),
        cost_estimate=pl.CostEstimate(flops=6 * 1024 * CELLS * 128, bytes_accessed=2000000, transcendentals=0),
        name="inverse_density",
    )(records, targets, slots, jnp.asarray(token, jnp.int32)[None], *(jnp.asarray(v, BF) for v in (row_tile, own_cell, tap)))


def grid_kernel(swath_ref, pos_ref, center_ref, out_ref):
    channels = swath_ref.shape[1]
    gap = jnp.zeros((TAPS, 8, FP), F32)

    def step(tiles_ref):
        i = pl.program_id(0)
        blocks = []
        for pair in range(2):
            first, second = 4 * i + 2 * pair, 4 * i + 2 * pair + 1
            left = weights_at(pos_ref[first].astype(F32), center_ref, 0).reshape(TAPS, 16, FP)
            right = weights_at(pos_ref[second].astype(F32), center_ref, 2).reshape(TAPS, 16, FP)
            left = jnp.concatenate([left, gap], 1).reshape(TAPS * PAIR, FP)
            right = jnp.concatenate([gap, right], 1).reshape(TAPS * PAIR, FP)
            table = jnp.concatenate([left, right], 1).astype(BF)
            data = jnp.concatenate([tiles_ref[2 * pair], tiles_ref[2 * pair + 1]], 1)
            total = lax.dot_general(table, data, NT, preferred_element_type=F32)
            blocks.append(total.reshape(TAPS, PAIR, channels))
        base = pl.multiple_of(i * 2 * PAIR, 2 * PAIR)
        out_ref[:, pl.ds(base, 2 * PAIR), :] = jnp.concatenate(blocks, 1).astype(BF)

    pltpu.emit_pipeline(
        step, grid=(TILES // 4,), in_specs=[pl.BlockSpec((4, channels, FP), lambda i: (i, 0, 0))]
    )(swath_ref)


def gridded(swath, pos, center):
    channels = swath.shape[1]
    vmem = pl.BlockSpec(memory_space=pltpu.VMEM)
    return pl.pallas_call(
        grid_kernel,
        in_specs=[pl.BlockSpec(memory_space=pl.ANY), vmem, vmem],
        out_specs=vmem,
        out_shape=pltpu.VMEM((TAPS, TILES * TPS, channels), BF),
        compiler_params=pltpu.CompilerParams(vmem_limit_bytes=KERNEL_VMEM),
        cost_estimate=pl.CostEstimate(
            flops=2 * (TILES // 2) * TAPS * PAIR * 2 * FP * 768,
            bytes_accessed=TILES * channels * FP * 2,
            transcendentals=TILES * FP * 256,
        ),
        name="grid_tiles",
    )(swath, pos, center)


def embed_kernel(own_ref, sib_ref, w0, w1, w2, w3, w4, inverse_ref, column_ref, row_ref, out_ref, total, spread):
    channels = own_ref.shape[2]
    slot_rows, half = out_ref.shape[0], own_ref.shape[1]
    part = slot_rows // TAPS
    width = total.shape[1]
    total[...] = jnp.zeros_like(total)

    def tap(k, carry):
        weight = jnp.concatenate([w[:, k].reshape(-1, channels) for w in (w0, w1, w2, w3, w4)], 0)
        scale = jnp.broadcast_to(inverse_ref[pl.ds(k, 1), :], (FP, 2 * half)).T
        scale = jnp.concatenate([scale] * (width // FP), 1)
        for n, ref in enumerate((own_ref, sib_ref)):
            rows = slice(n * half, (n + 1) * half)
            product = lax.dot_general(ref[k], weight, NT, preferred_element_type=F32)
            total[rows] += product * scale[rows]
        base = pl.multiple_of(k * part, part)
        here = lax.broadcasted_iota(jnp.int32, (part, 2 * half), 0) + base
        spread[pl.ds(base, part), :] = jnp.where(here == row_ref[...], 1.0, 0.0).astype(BF)
        return carry

    lax.fori_loop(0, TAPS, tap, 0)
    columns = lax.broadcasted_iota(jnp.int32, (width, width), 0)
    order = jnp.where(columns == column_ref[...], 1.0, 0.0).astype(BF)
    tokens = lax.dot_general(total[...].astype(BF), order, NT, preferred_element_type=F32).astype(BF)
    out_ref[...] = jnp.dot(spread[...], tokens, preferred_element_type=F32).astype(BF)


def embed(own, sib, weights, inverse, columns, rows):
    width = CHIPS * weights[0].shape[2]
    slot_rows = 2 * CHIPS * SLOTS * TPS
    half = TILES * TPS
    vmem = pl.BlockSpec(memory_space=pltpu.VMEM)
    large = [pltpu.with_memory_space_constraint(a, pltpu.VMEM) for a in (own, sib, *weights)]
    return pl.pallas_call(
        embed_kernel,
        in_specs=[vmem] * (len(large) + 3),
        out_specs=vmem,
        out_shape=jax.ShapeDtypeStruct((slot_rows, width), BF),
        scratch_shapes=[pltpu.VMEM((2 * half, width), F32), pltpu.VMEM((slot_rows, 2 * half), BF)],
        compiler_params=pltpu.CompilerParams(vmem_limit_bytes=KERNEL_VMEM),
        cost_estimate=pl.CostEstimate(flops=2 * TAPS * 2 * half * 768 * width * 2, bytes_accessed=1000000, transcendentals=0),
        name="embed_tiles",
    )(*large, inverse, columns, rows)


def attend_kernel(tokens_ref, row_ref, bias_ref, gain_ref, kv_ref, latent_ref, out_ref):
    rows = TPS * PATCHES
    per_core = tokens_ref.shape[0] * tokens_ref.shape[2]
    width = 2 * tokens_ref.shape[3]
    hot = lax.broadcasted_iota(jnp.int32, (rows, per_core), 0) == row_ref[...]
    hot = jnp.where(hot, 1.0, 0.0).astype(BF)
    halves = [
        jnp.dot(hot, tokens_ref[:, c].reshape(per_core, width // 2), preferred_element_type=F32) for c in range(2)
    ]
    tokens = (jnp.concatenate(halves, 1) + bias_ref[...]).astype(BF).astype(F32)
    mean = jnp.mean(tokens, axis=1, keepdims=True)
    shifted = tokens - mean
    var = jnp.mean(shifted * shifted, axis=1, keepdims=True)
    normed = (shifted * lax.rsqrt(var + 1e-05) * gain_ref[...]).astype(BF)
    keys_values = jnp.dot(normed, kv_ref[...], preferred_element_type=F32).astype(BF)
    keys, values = keys_values[:, :width], keys_values[:, width:].astype(F32)
    head = lax.broadcasted_iota(jnp.int32, (HEADS, width), 0)
    lane_head = lax.shift_right_logical(lax.broadcasted_iota(jnp.int32, (HEADS, width), 1), int(math.log2(HD)))
    query = jnp.concatenate(
        [jnp.where(head == lane_head, jnp.broadcast_to(latent_ref[l : l + 1], (HEADS, width)), 0.0) for l in range(LEVELS)],
        0,
    )
    scores = jnp.zeros((rows, LEVELS * HEADS), F32)
    for _ in range(3):
        piece = query.astype(BF)
        scores += lax.dot_general(keys, piece, NT, preferred_element_type=F32)
        query = query - piece.astype(F32)
    scores = (scores * (1.0 / math.sqrt(HD))).reshape(TPS, PATCHES, LEVELS * HEADS)
    top = jnp.max(scores, axis=0)
    expo = jnp.exp(scores - top[None])
    mass = jnp.sum(expo, axis=0)
    expo = expo.reshape(rows, LEVELS * HEADS).astype(BF)
    values = values.reshape(TPS, PATCHES, width)
    parts = []
    for value, count in ((top, 3), (mass, 2)):
        for _ in range(count):
            piece = value.astype(BF)
            parts.append(piece)
            value = value - piece.astype(F32)
    pick = lax.broadcasted_iota(jnp.int32, (LEVELS * HEADS, width), 0)
    stat_row = lax.broadcasted_iota(jnp.int32, (LEVELS * HEADS, FP), 0)
    stat_lane = lax.broadcasted_iota(jnp.int32, (LEVELS * HEADS, FP), 1)
    lane = lax.shift_right_logical(lax.broadcasted_iota(jnp.int32, (LEVELS * HEADS, width), 1), int(math.log2(HD)))
    blocks = []
    for level in range(LEVELS):
        wide = jnp.where(pick == lane + level * HEADS, 1.0, 0.0).astype(BF)
        share = jnp.dot(expo, wide, preferred_element_type=F32).reshape(TPS, PATCHES, width)
        partial = jnp.sum(share * values, axis=0)
        stats = jnp.zeros((PATCHES, FP), F32)
        for n, piece in enumerate(parts):
            to = (stat_row - level * HEADS == stat_lane - n * HEADS) & (stat_row >= level * HEADS) & (stat_row < (level + 1) * HEADS)
            stats += jnp.dot(piece, jnp.where(to, 1.0, 0.0).astype(BF), preferred_element_type=F32)
        blocks.append(jnp.concatenate([partial, stats], 1).astype(BF))
    stacked = jnp.concatenate(blocks, 0)
    count = LEVELS * PATCHES
    target = lax.broadcasted_iota(jnp.int32, (count, count), 0)
    source = lax.broadcasted_iota(jnp.int32, (count, count), 1)
    moved = (target & (LEVELS - 1)) * PATCHES + lax.shift_right_logical(target, 2) == source
    out_ref[...] = jnp.dot(jnp.where(moved, 1.0, 0.0).astype(BF), stacked, preferred_element_type=F32).astype(BF)


def attend(tokens, rows, bias, gain, kv_weight, latents):
    width = kv_weight.shape[0]
    return pl.pallas_call(
        attend_kernel,
        out_shape=jax.ShapeDtypeStruct((PATCHES * LEVELS, width + FP), BF),
        compiler_params=pltpu.CompilerParams(vmem_limit_bytes=KERNEL_VMEM),
        cost_estimate=pl.CostEstimate(flops=2 * 384 * 512 * 4000, bytes_accessed=3000000, transcendentals=12288),
        name="attend_source",
    )(tokens, rows, bias, gain, kv_weight, latents)


def finish_kernel(parts_ref, weight_ref, out_ref):
    sources, rows, wide = parts_ref.shape
    width = wide - FP
    stats = parts_ref[:, :, width:].reshape(sources * rows, FP)
    row = lax.broadcasted_iota(jnp.int32, (FP, width), 0)
    head = lax.shift_right_logical(lax.broadcasted_iota(jnp.int32, (FP, width), 1), int(math.log2(HD)))
    same = (row & (HEADS - 1)) == head
    is_top = jnp.where(same & (row < 3 * HEADS), 1.0, 0.0).astype(BF)
    is_mass = jnp.where(same & (row >= 3 * HEADS) & (row < 5 * HEADS), 1.0, 0.0).astype(BF)
    top = jnp.dot(stats, is_top, preferred_element_type=F32).reshape(sources, rows, width)
    mass = jnp.dot(stats, is_mass, preferred_element_type=F32).reshape(sources, rows, width)
    scale = jnp.exp(top - jnp.max(top, axis=0)[None])
    above = jnp.sum(scale * parts_ref[:, :, :width].astype(F32), axis=0)
    attended = (above / jnp.sum(scale * mass, axis=0)).astype(BF)
    result = jnp.dot(attended, weight_ref[...], preferred_element_type=F32)
    for patch in range(rows // LEVELS):
        out_ref[patch] = result[patch * LEVELS : (patch + 1) * LEVELS]


def finish(parts, out_weight):
    return pl.pallas_call(
        finish_kernel,
        out_shape=jax.ShapeDtypeStruct((parts.shape[1] // LEVELS, LEVELS, out_weight.shape[1]), F32),
        cost_estimate=pl.CostEstimate(flops=2 * 128 * 128 * 1024, bytes_accessed=800000, transcendentals=65536),
        name="combine_sources",
    )(parts, out_weight)


def device_at(y, x, core):
    return ((y % SIDE) * SIDE + x % SIDE) * 2 + core


def shift(offset, second):
    pairs = []
    for y in range(SIDE):
        for x in range(SIDE):
            for core in range(2):
                along_x = (core == 0) != second
                to = device_at(y, x + offset, core) if along_x else device_at(y + offset, x, core)
                pairs.append((device_at(y, x, core), to))
    return pairs


def send(array, offset, second):
    return lax.ppermute(array, "lat", shift(offset, second))


def gather(shard, record, swap):
    half = TAPS // 2
    up, down = send(shard, 1, False), send(shard, -1, False)
    others = [send(record, -offset, False) for offset in OFFSETS[1:]]
    up, down, *others = lax.optimization_barrier((up, down, *others))
    record = jnp.stack([record] + others, 0)
    far = [send(up[:half], 1, False), send(down[half:], -1, False)]
    others = [send(record, -offset, True) for offset in OFFSETS[1:]]
    *far, others = lax.optimization_barrier((*far, others))
    record = jnp.stack([record] + others, 0)
    line = jnp.stack([shard, up, down, jnp.concatenate(far, 0)], 0)
    above, below = send(line, 1, True), send(line, -1, True)
    sib_record = lax.ppermute(record, "lat", swap)
    weights = [line, above, below, send(above[:2], 1, True), send(below[2:], -1, True)]
    return weights, record, sib_record


def offset_at(index):
    return jnp.where(index == 0, 0, jnp.where(index == 1, -1, index - 1))


def index_of(offset):
    offset = offset % SIDE
    return jnp.where(offset == 0, 0, jnp.where(offset == SIDE - 1, 1, offset + 1))


def body(
    swath,
    tile_band,
    tile_patch,
    fp_pos,
    conv_weight,
    conv_bias,
    norm_gain,
    latents,
    kv_weight,
    out_weight,
):
    place = lax.axis_index("lat")
    core, chip = place % 2, place // 2
    chip_y, chip_x = chip // SIDE, chip % SIDE
    swath, fp_pos = swath[0], fp_pos[0]
    channels, cols = swath.shape[1], conv_weight.shape[4]
    width = kv_weight.shape[0]
    swap = [(i, i ^ 1) for i in range(2 * CHIPS)]

    shard = jnp.transpose(conv_weight[0].reshape(TAPS, channels, cols), (0, 2, 1))
    record = tile_records(tile_band[0, :, 0], tile_patch[0], fp_pos)
    weights, record, sib_record = gather(shard, record, swap)
    sib_swath = lax.ppermute(swath, "lat", swap)
    sib_pos = lax.ppermute(fp_pos, "lat", swap)
    center = jnp.asarray(
        np.concatenate([centers(list(range(TPS)) + [-1] * 4), centers([-1] * 4 + list(ROW_TOKEN[TPS:]))], 0)
    )
    swath, sib_swath, _, _ = lax.optimization_barrier((swath, sib_swath, weights[1], weights[2]))
    own = gridded(swath, fp_pos, center)
    sib = gridded(sib_swath, sib_pos, center)
    records = jnp.stack([record, sib_record]).reshape(2, CHIPS, TILES, RECORD)
    about = records[:, 0, :, CELLS : CELLS + 2].astype(jnp.int32)
    bands_here = about[:, :, 0]
    targets = (bands_here * PATCHES + about[:, :, 1]).reshape(1, -1).astype(F32)
    earlier = jnp.asarray(np.tril(np.ones((TILES, TILES), np.int32), -1))
    rank = jnp.sum((bands_here[:, :, None] == bands_here[:, None, :]).astype(jnp.int32) * earlier, axis=2)
    origin = jnp.stack([core, 1 - core])[:, None]
    slots = (bands_here * SLOTS + 2 * origin + rank).reshape(1, -1).astype(F32)
    inverse, rows = inverse_density(records.reshape(-1, RECORD), targets, slots)

    column = jnp.arange(CHIPS * cols, dtype=jnp.int32)[None, :]
    near, farther = offset_at(column // cols % SIDE), offset_at(column // cols // SIDE)
    at_y = (chip_y + jnp.where(core == 0, farther, near)) % SIDE
    at_x = (chip_x + jnp.where(core == 0, near, farther)) % SIDE
    columns = (at_y * SIDE + at_x) * cols + column % cols
    outgoing = embed(own, sib, weights, inverse, columns.astype(jnp.int32), rows)

    outgoing = outgoing.reshape(2 * CHIPS, SLOTS * TPS, CHIPS * cols)
    incoming = lax.all_to_all(outgoing, "lat", split_axis=0, concat_axis=0, tiled=True)
    mine = records[:, :, :, CELLS].astype(F32) == place.astype(F32)
    patches = jnp.where(mine, records[:, :, :, CELLS + 1].astype(F32) + 1, 0)
    before = jnp.einsum("cdt,tu->cdu", mine.astype(F32), jnp.asarray(np.triu(np.ones((TILES, TILES), np.float32), 1)))
    patch_at = jnp.stack([jnp.sum(jnp.where(before == n, patches, 0), axis=2) for n in range(2)], 2)
    number = jnp.arange(CHIPS)
    in_y, in_x = index_of(number // SIDE - chip_y), index_of(number % SIDE - chip_x)
    x_first, y_first = SIDE * in_y + in_x, SIDE * in_x + in_y
    order = jnp.stack([jnp.where(core == 0, x_first, y_first), jnp.where(core == 0, y_first, x_first)])
    hot = (order[:, :, None] == number[None, None, :]).astype(F32)
    patch_by = jnp.einsum("cnd,cdk->nck", hot, patch_at)
    patch_by = jnp.where(core == 0, patch_by, patch_by[:, ::-1])
    patch_in = patch_by.astype(jnp.int32).reshape(-1, 1) - 1
    token_in = jnp.where(patch_in < 0, -1, patch_in + PATCHES * jnp.arange(TPS)[None, :]).reshape(1, -1)

    def by_core(array):
        shape = array.shape[1:]
        split = array.reshape((CHIPS, 2, cols) + shape)
        return jnp.swapaxes(split, 0, 1).reshape((width,) + shape)

    parts = attend(
        incoming.reshape(CHIPS, 2, SLOTS * TPS, CHIPS * cols),
        token_in.astype(jnp.int32),
        by_core(conv_bias[0])[None],
        by_core(norm_gain)[None],
        by_core(kv_weight),
        latents,
    )
    sources = lax.axis_size("src")
    parts = lax.all_to_all(
        parts.reshape(sources, -1, width + FP), "src", split_axis=0, concat_axis=0, tiled=True
    )
    return finish(parts, out_weight)


def solution(mesh):
    in_specs = (
        P("src", "lat", None, None),
        P("src", "lat", None),
        P("src", "lat"),
        P("src", "lat", None, None),
        P("src", None, None, None, "lat"),
        P("src", None),
        P(),
        P(),
        P(),
        P(),
    )
    out_specs = P(("lat", "src"), None, None)
    return jax.shard_map(body, mesh=mesh, in_specs=in_specs, out_specs=out_specs, check_vma=False)
```

```python
import math

import jax
import jax.numpy as jnp
import numpy as np
from jax import lax
from jax.experimental import pallas as pl
from jax.experimental.pallas import tpu as pltpu
from jax.sharding import PartitionSpec as P

HEADS = 8
HD = 64
PW = 24
KS = 4
TPS = 12
LEVELS = 4
TILES = 32
PATCHES = 32
CHIPS = 16
SIDE = 4
CELLS = 192
TAPS = KS * KS
SLOTS = 4
FP = 128
PAIR = 2 * TPS
FAR = 1.0e4
OFFSETS = (0, -1, 1, 2)
ROW_TOKEN = np.array(list(range(TPS)) + [8, 9, 10, 11, 0, 1, 2, 3, 4, 5, 6, 7])
BF = jnp.bfloat16
F32 = jnp.float32
NT = (((1,), (1,)), ((), ()))
KERNEL_VMEM = 24 * 2**20
RECORD = 256
SMALL = pl.CostEstimate(flops=1000000, bytes_accessed=10000, transcendentals=0)


def centers(tokens):
    rows, cols = [], []
    for tap in range(TAPS):
        for token in tokens:
            rows.append(token // 6 * KS + tap // KS + 0.5 if token >= 0 else FAR)
            cols.append(token % 6 * KS + tap % KS + 0.5 if token >= 0 else FAR)
    wide = [np.repeat(np.array(v, np.float32)[:, None], FP, 1) for v in (rows, cols)]
    return np.stack(wide)


def weights_at(pos, center_ref, index):
    down = pos[0:1] - center_ref[index]
    across = pos[1:2] - center_ref[index + 1]
    return jnp.exp((down * down + across * across) * (-1.0 / 1.125))


def record_kernel(band_ref, patch_ref, pos_ref, center_ref, out_ref):
    ones = jnp.ones((8, FP), BF)
    place = lax.broadcasted_iota(jnp.int32, (8, RECORD), 0)
    lane = lax.broadcasted_iota(jnp.int32, (8, RECORD - CELLS), 1)

    def group(g, carry):
        base = pl.multiple_of(g * 8, 8)
        total = jnp.zeros((8, RECORD), F32)
        for j in range(8):
            table = weights_at(pos_ref[base + j].astype(F32), center_ref, 0).astype(BF)
            row = lax.dot_general(ones, table, NT, preferred_element_type=F32)
            about = jnp.where(lane == 0, band_ref[base + j], patch_ref[base + j]).astype(F32)
            total = jnp.where(place == j, jnp.concatenate([row, about], 1), total)
        return carry + (total,)

    rows = ()
    for g in range(TILES // 8):
        rows = group(g, rows)
    out_ref[...] = jnp.concatenate(rows, 0).astype(BF)


def tile_records(band, patch, pos):
    vmem, smem = pl.BlockSpec(memory_space=pltpu.VMEM), pl.BlockSpec(memory_space=pltpu.SMEM)
    return pl.pallas_call(
        record_kernel,
        in_specs=[smem, smem, vmem, vmem],
        out_shape=jax.ShapeDtypeStruct((TILES, RECORD), BF),
        cost_estimate=SMALL,
        name="tile_records",
    )(band, patch, pos, jnp.asarray(centers(range(TPS))))


def inverse_kernel(core_ref, own_ref, sib_ref, token_ref, row_tile_ref, own_cell_ref, tap_ref, out_ref, row_ref):
    here = 2 * TILES

    def as_row(column):
        return jnp.broadcast_to(column, (column.shape[0], FP)).T[:1]

    about = jnp.concatenate([own_ref[:TILES, CELLS:], sib_ref[:TILES, CELLS:]], 0).astype(F32)
    band, target = about[:, :1], about[:, :1] * PATCHES + about[:, 1:2]
    band_row, target_row = as_row(band), as_row(target)
    total = jnp.ones((CELLS, here), F32)
    for ref in (own_ref, sib_ref):
        about = ref[:, CELLS:].astype(F32)
        same = jnp.where(about[:, :1] * PATCHES + about[:, 1:2] == target_row, 1.0, 0.0).astype(BF)
        total += lax.dot_general(ref[:, :CELLS], same, (((0,), (0,)), ((), ())), preferred_element_type=F32)
    inverse = 1.0 / total
    out = jnp.zeros(out_ref.shape, F32)
    for _ in range(3):
        piece = inverse.astype(BF)
        spread = jnp.dot(piece, row_tile_ref[...], preferred_element_type=F32).astype(BF) * own_cell_ref[...]
        out += jnp.dot(tap_ref[...], spread, preferred_element_type=F32)
        inverse = inverse - piece.astype(F32)
    out_ref[...] = out
    other = lax.broadcasted_iota(jnp.int32, (here, here), 0)
    tile = lax.broadcasted_iota(jnp.int32, (here, here), 1)
    earlier = (other < tile) & ((other < TILES) == (tile < TILES)) & (band == band_row)
    rank = jnp.sum(jnp.where(earlier, 1.0, 0.0), axis=0, keepdims=True)
    origin = jnp.where(tile[:1] < TILES, core_ref[0], 1 - core_ref[0]).astype(F32)
    slots = jnp.broadcast_to(band_row * SLOTS + 2 * origin + rank, (8, here)).astype(BF)
    slots = jnp.dot(slots, row_tile_ref[...], preferred_element_type=F32)
    row_ref[...] = slots[:1].astype(jnp.int32) * TPS + token_ref[...]


def inverse_density(core, own, sib):
    rows = 2 * TILES * TPS
    row_tile = (np.arange(2 * TILES)[:, None] == np.arange(rows)[None, :] // TPS).astype(np.float32)
    token = np.tile(ROW_TOKEN, TILES)
    own_cell = (np.arange(CELLS)[:, None] % TPS == token[None, :]).astype(np.float32)
    tap = (np.arange(TAPS)[:, None] == np.arange(CELLS)[None, :] // TPS).astype(np.float32)
    vmem, smem = pl.BlockSpec(memory_space=pltpu.VMEM), pl.BlockSpec(memory_space=pltpu.SMEM)
    return pl.pallas_call(
        inverse_kernel,
        in_specs=[smem] + [vmem] * 6,
        out_shape=(jax.ShapeDtypeStruct((TAPS, rows), F32), jax.ShapeDtypeStruct((1, rows), jnp.int32)),
        compiler_params=pltpu.CompilerParams(vmem_limit_bytes=KERNEL_VMEM // 2),
        cost_estimate=SMALL,
        name="inverse_density",
    )(core, own, sib, jnp.asarray(token, jnp.int32)[None], *(jnp.asarray(v, BF) for v in (row_tile, own_cell, tap)))


def grid_kernel(swath_ref, pos_ref, center_ref, out_ref):
    channels = swath_ref.shape[1]
    gap = jnp.zeros((TAPS, 8, FP), F32)

    def step(tiles_ref):
        i = pl.program_id(0)
        blocks = []
        for pair in range(2):
            first, second = 4 * i + 2 * pair, 4 * i + 2 * pair + 1
            left = weights_at(pos_ref[first].astype(F32), center_ref, 0).reshape(TAPS, 16, FP)
            right = weights_at(pos_ref[second].astype(F32), center_ref, 2).reshape(TAPS, 16, FP)
            left = jnp.concatenate([left, gap], 1).reshape(TAPS * PAIR, FP)
            right = jnp.concatenate([gap, right], 1).reshape(TAPS * PAIR, FP)
            table = jnp.concatenate([left, right], 1).astype(BF)
            data = jnp.concatenate([tiles_ref[2 * pair], tiles_ref[2 * pair + 1]], 1)
            total = lax.dot_general(table, data, NT, preferred_element_type=F32)
            blocks.append(total.reshape(TAPS, PAIR, channels))
        base = pl.multiple_of(i * 2 * PAIR, 2 * PAIR)
        out_ref[:, pl.ds(base, 2 * PAIR), :] = jnp.concatenate(blocks, 1).astype(BF)

    pltpu.emit_pipeline(
        step, grid=(TILES // 4,), in_specs=[pl.BlockSpec((4, channels, FP), lambda i: (i, 0, 0))]
    )(swath_ref)


def gridded(swath, pos, center):
    channels = swath.shape[1]
    vmem = pl.BlockSpec(memory_space=pltpu.VMEM)
    swath = pltpu.with_memory_space_constraint(swath, pltpu.HBM)
    return pl.pallas_call(
        grid_kernel,
        in_specs=[pl.BlockSpec(memory_space=pl.ANY), vmem, vmem],
        out_specs=vmem,
        out_shape=pltpu.VMEM((TAPS, TILES * TPS, channels), BF),
        compiler_params=pltpu.CompilerParams(vmem_limit_bytes=KERNEL_VMEM // 2),
        cost_estimate=SMALL,
        name="grid_tiles",
    )(swath, pos, center)


def embed_kernel(own_ref, sib_ref, *refs):
    *weight_refs, inverse_ref, column_ref, row_ref, out_ref, total, spread = refs
    channels = own_ref.shape[2]
    slot_rows, half = out_ref.shape[0], own_ref.shape[1]
    part = slot_rows // TAPS
    width = total.shape[1]
    total[...] = jnp.zeros_like(total)

    def tap(k, carry):
        weight = jnp.concatenate([w[:, k].reshape(-1, channels) for w in weight_refs], 0)
        scale = jnp.broadcast_to(inverse_ref[pl.ds(k, 1), :], (FP, 2 * half)).T
        scale = jnp.concatenate([scale] * (width // FP), 1)
        for n, ref in enumerate((own_ref, sib_ref)):
            rows = slice(n * half, (n + 1) * half)
            product = lax.dot_general(ref[k], weight, NT, preferred_element_type=F32)
            total[rows] += product * scale[rows]
        base = pl.multiple_of(k * part, part)
        here = lax.broadcasted_iota(jnp.int32, (part, 2 * half), 0) + base
        spread[pl.ds(base, part), :] = jnp.where(here == row_ref[...], 1.0, 0.0).astype(BF)
        return carry

    lax.fori_loop(0, TAPS, tap, 0)
    columns = lax.broadcasted_iota(jnp.int32, (width, width), 0)
    order = jnp.where(columns == column_ref[...], 1.0, 0.0).astype(BF)
    tokens = lax.dot_general(total[...].astype(BF), order, NT, preferred_element_type=F32).astype(BF)
    out_ref[...] = jnp.dot(spread[...], tokens, preferred_element_type=F32).astype(BF)


def embed(own, sib, weights, inverse, columns, rows):
    width = CHIPS * weights[0].shape[2]
    slot_rows = 2 * CHIPS * SLOTS * TPS
    half = TILES * TPS
    vmem = pl.BlockSpec(memory_space=pltpu.VMEM)
    large = [pltpu.with_memory_space_constraint(a, pltpu.VMEM) for a in (own, sib, *weights)]
    return pl.pallas_call(
        embed_kernel,
        in_specs=[vmem] * (len(large) + 3),
        out_specs=vmem,
        out_shape=jax.ShapeDtypeStruct((slot_rows, width), BF),
        scratch_shapes=[pltpu.VMEM((2 * half, width), F32), pltpu.VMEM((slot_rows, 2 * half), BF)],
        compiler_params=pltpu.CompilerParams(vmem_limit_bytes=KERNEL_VMEM // 2),
        cost_estimate=pl.CostEstimate(flops=2 * TAPS * 2 * half * 768 * width * 2, bytes_accessed=1000000, transcendentals=0),
        name="embed_tiles",
    )(*large, inverse, columns, rows)


def attend_kernel(tokens_ref, row_ref, bias_ref, gain_ref, kv_ref, latent_ref, out_ref):
    rows = TPS * PATCHES
    per_core = tokens_ref.shape[0] * tokens_ref.shape[2]
    width = 2 * tokens_ref.shape[3]
    hot = lax.broadcasted_iota(jnp.int32, (rows, per_core), 0) == row_ref[...]
    hot = jnp.where(hot, 1.0, 0.0).astype(BF)
    halves = [
        jnp.dot(hot, tokens_ref[:, c].reshape(per_core, width // 2), preferred_element_type=F32) for c in range(2)
    ]
    tokens = (jnp.concatenate(halves, 1) + bias_ref[...]).astype(BF).astype(F32)
    mean = jnp.mean(tokens, axis=1, keepdims=True)
    shifted = tokens - mean
    var = jnp.mean(shifted * shifted, axis=1, keepdims=True)
    normed = (shifted * lax.rsqrt(var + 1e-05) * gain_ref[...]).astype(BF)
    keys_values = jnp.dot(normed, kv_ref[...], preferred_element_type=F32).astype(BF)
    keys, values = keys_values[:, :width], keys_values[:, width:].astype(F32)
    head = lax.broadcasted_iota(jnp.int32, (HEADS, width), 0)
    lane_head = lax.shift_right_logical(lax.broadcasted_iota(jnp.int32, (HEADS, width), 1), int(math.log2(HD)))
    query = jnp.concatenate(
        [jnp.where(head == lane_head, jnp.broadcast_to(latent_ref[l : l + 1], (HEADS, width)), 0.0) for l in range(LEVELS)],
        0,
    )
    scores = jnp.zeros((rows, LEVELS * HEADS), F32)
    for _ in range(3):
        piece = query.astype(BF)
        scores += lax.dot_general(keys, piece, NT, preferred_element_type=F32)
        query = query - piece.astype(F32)
    scores = (scores * (1.0 / math.sqrt(HD))).reshape(TPS, PATCHES, LEVELS * HEADS)
    top = jnp.max(scores, axis=0)
    expo = jnp.exp(scores - top[None])
    mass = jnp.sum(expo, axis=0)
    expo = expo.reshape(rows, LEVELS * HEADS).astype(BF)
    values = values.reshape(TPS, PATCHES, width)
    parts = []
    for value, count in ((top, 3), (mass, 2)):
        for _ in range(count):
            piece = value.astype(BF)
            parts.append(piece)
            value = value - piece.astype(F32)
    pick = lax.broadcasted_iota(jnp.int32, (LEVELS * HEADS, width), 0)
    stat_row = lax.broadcasted_iota(jnp.int32, (LEVELS * HEADS, FP), 0)
    stat_lane = lax.broadcasted_iota(jnp.int32, (LEVELS * HEADS, FP), 1)
    lane = lax.shift_right_logical(lax.broadcasted_iota(jnp.int32, (LEVELS * HEADS, width), 1), int(math.log2(HD)))
    blocks = []
    for level in range(LEVELS):
        wide = jnp.where(pick == lane + level * HEADS, 1.0, 0.0).astype(BF)
        share = jnp.dot(expo, wide, preferred_element_type=F32).reshape(TPS, PATCHES, width)
        partial = jnp.sum(share * values, axis=0)
        stats = jnp.zeros((PATCHES, FP), F32)
        for n, piece in enumerate(parts):
            to = (stat_row - level * HEADS == stat_lane - n * HEADS) & (stat_row >= level * HEADS) & (stat_row < (level + 1) * HEADS)
            stats += jnp.dot(piece, jnp.where(to, 1.0, 0.0).astype(BF), preferred_element_type=F32)
        blocks.append(jnp.concatenate([partial, stats], 1).astype(BF))
    stacked = jnp.concatenate(blocks, 0)
    count = LEVELS * PATCHES
    target = lax.broadcasted_iota(jnp.int32, (count, count), 0)
    source = lax.broadcasted_iota(jnp.int32, (count, count), 1)
    moved = (target & (LEVELS - 1)) * PATCHES + lax.shift_right_logical(target, 2) == source
    out_ref[...] = jnp.dot(jnp.where(moved, 1.0, 0.0).astype(BF), stacked, preferred_element_type=F32).astype(BF)


def attend(tokens, rows, bias, gain, kv_weight, latents):
    width = kv_weight.shape[0]
    return pl.pallas_call(
        attend_kernel,
        out_shape=jax.ShapeDtypeStruct((PATCHES * LEVELS, width + FP), BF),
        compiler_params=pltpu.CompilerParams(vmem_limit_bytes=KERNEL_VMEM),
        cost_estimate=pl.CostEstimate(flops=2 * 384 * 512 * 4000, bytes_accessed=3000000, transcendentals=12288),
        name="attend_source",
    )(tokens, rows, bias, gain, kv_weight, latents)


def finish_kernel(parts_ref, weight_ref, out_ref):
    sources, rows, wide = parts_ref.shape
    width = wide - FP
    stats = parts_ref[:, :, width:].reshape(sources * rows, FP)
    row = lax.broadcasted_iota(jnp.int32, (FP, width), 0)
    head = lax.shift_right_logical(lax.broadcasted_iota(jnp.int32, (FP, width), 1), int(math.log2(HD)))
    same = (row & (HEADS - 1)) == head
    is_top = jnp.where(same & (row < 3 * HEADS), 1.0, 0.0).astype(BF)
    is_mass = jnp.where(same & (row >= 3 * HEADS) & (row < 5 * HEADS), 1.0, 0.0).astype(BF)
    top = jnp.dot(stats, is_top, preferred_element_type=F32).reshape(sources, rows, width)
    mass = jnp.dot(stats, is_mass, preferred_element_type=F32).reshape(sources, rows, width)
    scale = jnp.exp(top - jnp.max(top, axis=0)[None])
    above = jnp.sum(scale * parts_ref[:, :, :width].astype(F32), axis=0)
    attended = (above / jnp.sum(scale * mass, axis=0)).astype(BF)
    result = jnp.dot(attended, weight_ref[...], preferred_element_type=F32)
    for patch in range(rows // LEVELS):
        out_ref[patch] = result[patch * LEVELS : (patch + 1) * LEVELS]


def finish(parts, out_weight):
    return pl.pallas_call(
        finish_kernel,
        out_shape=jax.ShapeDtypeStruct((parts.shape[1] // LEVELS, LEVELS, out_weight.shape[1]), F32),
        cost_estimate=pl.CostEstimate(flops=2 * 128 * 128 * 1024, bytes_accessed=800000, transcendentals=65536),
        name="combine_sources",
    )(parts, out_weight)


def device_at(y, x, core):
    return ((y % SIDE) * SIDE + x % SIDE) * 2 + core


def shift(offset, second):
    pairs = []
    for y in range(SIDE):
        for x in range(SIDE):
            for core in range(2):
                along_x = (core == 0) != second
                to = device_at(y, x + offset, core) if along_x else device_at(y + offset, x, core)
                pairs.append((device_at(y, x, core), to))
    return pairs


def send(array, offset, second):
    return lax.ppermute(array, "lat", shift(offset, second))


def offset_at(index):
    return jnp.where(index == 0, 0, jnp.where(index == 1, -1, index - 1))


def index_of(offset):
    offset = offset % SIDE
    return jnp.where(offset == 0, 0, jnp.where(offset == SIDE - 1, 1, offset + 1))


def body(
    swath,
    tile_band,
    tile_patch,
    fp_pos,
    conv_weight,
    conv_bias,
    norm_gain,
    latents,
    kv_weight,
    out_weight,
):
    place = lax.axis_index("lat")
    core, chip = place % 2, place // 2
    chip_y, chip_x = chip // SIDE, chip % SIDE
    swath, fp_pos = swath[0], fp_pos[0]
    channels, cols = swath.shape[1], conv_weight.shape[4]
    width = kv_weight.shape[0]
    swap = [(i, i ^ 1) for i in range(2 * CHIPS)]

    shard = jnp.transpose(conv_weight[0].reshape(TAPS, channels, cols), (0, 2, 1))
    center = jnp.asarray(
        np.concatenate([centers(list(range(TPS)) + [-1] * 4), centers([-1] * 4 + list(ROW_TOKEN[TPS:]))], 0)
    )
    half = TAPS // 2
    up, down = send(shard, 1, False), send(shard, -1, False)
    sib_swath = lax.ppermute(swath, "lat", swap)
    sib_pos = lax.ppermute(fp_pos, "lat", swap)
    record = tile_records(tile_band[0, :, 0], tile_patch[0], fp_pos)
    up, down, record = lax.optimization_barrier((up, down, record))
    far = [send(up[:half], 1, False), send(down[half:], -1, False)]
    others = [send(record, -offset, False) for offset in OFFSETS[1:]]
    *far, record = lax.optimization_barrier((*far, jnp.stack([record] + others, 0)))
    low = jnp.stack([shard, up], 0)
    high = jnp.stack([down, jnp.concatenate(far, 0)], 0)
    above_low, below_high = send(low, 1, True), send(high, -1, True)
    record = jnp.stack([record] + [send(record, -offset, True) for offset in OFFSETS[1:]], 0)
    above_low, below_high, low, high, record, swath, sib_swath = lax.optimization_barrier(
        (above_low, below_high, low, high, record, swath, sib_swath)
    )
    corner_low, corner_high = send(above_low, 1, True), send(below_high, -1, True)
    above_high, below_low = send(high, 1, True), send(low, -1, True)
    sib_record = lax.ppermute(record, "lat", swap)
    own = gridded(swath, fp_pos, center)
    sib = gridded(sib_swath, sib_pos, center)
    weights = [low, high, above_low, above_high, below_low, below_high, corner_low, corner_high]

    inverse, rows = inverse_density(
        core[None].astype(jnp.int32), record.reshape(-1, RECORD), sib_record.reshape(-1, RECORD)
    )

    column = jnp.arange(CHIPS * cols, dtype=jnp.int32)[None, :]
    near, farther = offset_at(column // cols % SIDE), offset_at(column // cols // SIDE)
    at_y = (chip_y + jnp.where(core == 0, farther, near)) % SIDE
    at_x = (chip_x + jnp.where(core == 0, near, farther)) % SIDE
    columns = (at_y * SIDE + at_x) * cols + column % cols
    outgoing = embed(own, sib, weights, inverse, columns.astype(jnp.int32), rows)

    record, sib_record, conv_bias, norm_gain, kv_weight, outgoing = lax.optimization_barrier(
        (record, sib_record, conv_bias, norm_gain, kv_weight, outgoing)
    )
    about = jnp.stack([record[..., CELLS : CELLS + 2], sib_record[..., CELLS : CELLS + 2]])
    about = about.reshape(2, CHIPS, TILES, 2).astype(F32)
    outgoing = outgoing.reshape(2 * CHIPS, SLOTS * TPS, CHIPS * cols)
    incoming = lax.all_to_all(outgoing, "lat", split_axis=0, concat_axis=0, tiled=True)
    mine = about[..., 0] == place.astype(F32)
    patches = jnp.where(mine, about[..., 1] + 1, 0)
    before = jnp.einsum("cdt,tu->cdu", mine.astype(F32), jnp.asarray(np.triu(np.ones((TILES, TILES), np.float32), 1)))
    patch_at = jnp.stack([jnp.sum(jnp.where(before == n, patches, 0), axis=2) for n in range(2)], 2)
    number = jnp.arange(CHIPS)
    in_y, in_x = index_of(number // SIDE - chip_y), index_of(number % SIDE - chip_x)
    x_first, y_first = SIDE * in_y + in_x, SIDE * in_x + in_y
    order = jnp.stack([jnp.where(core == 0, x_first, y_first), jnp.where(core == 0, y_first, x_first)])
    hot = (order[:, :, None] == number[None, None, :]).astype(F32)
    patch_by = jnp.einsum("cnd,cdk->nck", hot, patch_at)
    patch_by = jnp.where(core == 0, patch_by, patch_by[:, ::-1])
    patch_in = patch_by.astype(jnp.int32).reshape(-1, 1) - 1
    token_in = jnp.where(patch_in < 0, -1, patch_in + PATCHES * jnp.arange(TPS)[None, :]).reshape(1, -1)

    def by_core(array):
        shape = array.shape[1:]
        split = array.reshape((CHIPS, 2, cols) + shape)
        return jnp.swapaxes(split, 0, 1).reshape((width,) + shape)

    parts = attend(
        incoming.reshape(CHIPS, 2, SLOTS * TPS, CHIPS * cols),
        token_in.astype(jnp.int32),
        by_core(conv_bias[0])[None],
        by_core(norm_gain)[None],
        by_core(kv_weight),
        latents,
    )
    sources = lax.axis_size("src")
    parts = lax.all_to_all(
        parts.reshape(sources, -1, width + FP), "src", split_axis=0, concat_axis=0, tiled=True
    )
    return finish(parts, out_weight)


def solution(mesh):
    in_specs = (
        P("src", "lat", None, None),
        P("src", "lat", None),
        P("src", "lat"),
        P("src", "lat", None, None),
        P("src", None, None, None, "lat"),
        P("src", None),
        P(),
        P(),
        P(),
        P(),
    )
    out_specs = P(("lat", "src"), None, None)
    return jax.shard_map(body, mesh=mesh, in_specs=in_specs, out_specs=out_specs, check_vma=False)
```

```python
import math

import jax
import jax.numpy as jnp
import numpy as np
from jax import lax
from jax.experimental import pallas as pl
from jax.experimental.pallas import tpu as pltpu
from jax.sharding import PartitionSpec as P

HEADS = 8
HD = 64
PW = 24
KS = 4
TPS = 12
LEVELS = 4
TILES = 32
PATCHES = 32
CHIPS = 16
SIDE = 4
CELLS = 192
TAPS = KS * KS
SLOTS = 4
FP = 128
PAIR = 2 * TPS
FAR = 1.0e4
OFFSETS = (0, -1, 1, 2)
ROW_TOKEN = np.array(list(range(TPS)) + [8, 9, 10, 11, 0, 1, 2, 3, 4, 5, 6, 7])
BF = jnp.bfloat16
F32 = jnp.float32
NT = (((1,), (1,)), ((), ()))
KERNEL_VMEM = 24 * 2**20
RECORD = 256
SMALL = pl.CostEstimate(flops=1000000, bytes_accessed=10000, transcendentals=0)


def centers(tokens):
    rows, cols = [], []
    for tap in range(TAPS):
        for token in tokens:
            rows.append(token // 6 * KS + tap // KS + 0.5 if token >= 0 else FAR)
            cols.append(token % 6 * KS + tap % KS + 0.5 if token >= 0 else FAR)
    wide = [np.repeat(np.array(v, np.float32)[:, None], FP, 1) for v in (rows, cols)]
    return np.stack(wide)


def weights_at(pos, center_ref, index):
    down = pos[0:1] - center_ref[index]
    across = pos[1:2] - center_ref[index + 1]
    return jnp.exp((down * down + across * across) * (-1.0 / 1.125))


def record_kernel(band_ref, patch_ref, pos_ref, center_ref, out_ref):
    ones = jnp.ones((8, FP), BF)
    place = lax.broadcasted_iota(jnp.int32, (8, RECORD), 0)
    lane = lax.broadcasted_iota(jnp.int32, (8, RECORD - CELLS), 1)

    def group(g, carry):
        base = pl.multiple_of(g * 8, 8)
        total = jnp.zeros((8, RECORD), F32)
        for j in range(8):
            table = weights_at(pos_ref[base + j].astype(F32), center_ref, 0).astype(BF)
            row = lax.dot_general(ones, table, NT, preferred_element_type=F32)
            about = jnp.where(lane == 0, band_ref[base + j], patch_ref[base + j]).astype(F32)
            total = jnp.where(place == j, jnp.concatenate([row, about], 1), total)
        return carry + (total,)

    rows = ()
    for g in range(TILES // 8):
        rows = group(g, rows)
    out_ref[...] = jnp.concatenate(rows, 0).astype(BF)


def tile_records(band, patch, pos):
    vmem, smem = pl.BlockSpec(memory_space=pltpu.VMEM), pl.BlockSpec(memory_space=pltpu.SMEM)
    return pl.pallas_call(
        record_kernel,
        in_specs=[smem, smem, vmem, vmem],
        out_shape=jax.ShapeDtypeStruct((TILES, RECORD), BF),
        cost_estimate=SMALL,
        name="tile_records",
    )(band, patch, pos, jnp.asarray(centers(range(TPS))))


def inverse_kernel(core_ref, own_ref, sib_ref, token_ref, row_tile_ref, own_cell_ref, tap_ref, out_ref, row_ref):
    here = 2 * TILES

    def as_row(column):
        return jnp.broadcast_to(column, (column.shape[0], FP)).T[:1]

    about = jnp.concatenate([own_ref[:TILES, CELLS:], sib_ref[:TILES, CELLS:]], 0).astype(F32)
    band, target = about[:, :1], about[:, :1] * PATCHES + about[:, 1:2]
    band_row, target_row = as_row(band), as_row(target)
    total = jnp.ones((CELLS, here), F32)
    for ref in (own_ref, sib_ref):
        about = ref[:, CELLS:].astype(F32)
        same = jnp.where(about[:, :1] * PATCHES + about[:, 1:2] == target_row, 1.0, 0.0).astype(BF)
        total += lax.dot_general(ref[:, :CELLS], same, (((0,), (0,)), ((), ())), preferred_element_type=F32)
    inverse = 1.0 / total
    out = jnp.zeros(out_ref.shape, F32)
    for _ in range(3):
        piece = inverse.astype(BF)
        spread = jnp.dot(piece, row_tile_ref[...], preferred_element_type=F32).astype(BF) * own_cell_ref[...]
        out += jnp.dot(tap_ref[...], spread, preferred_element_type=F32)
        inverse = inverse - piece.astype(F32)
    out_ref[...] = out
    other = lax.broadcasted_iota(jnp.int32, (here, here), 0)
    tile = lax.broadcasted_iota(jnp.int32, (here, here), 1)
    earlier = (other < tile) & ((other < TILES) == (tile < TILES)) & (band == band_row)
    rank = jnp.sum(jnp.where(earlier, 1.0, 0.0), axis=0, keepdims=True)
    origin = jnp.where(tile[:1] < TILES, core_ref[0], 1 - core_ref[0]).astype(F32)
    slots = jnp.broadcast_to(band_row * SLOTS + 2 * origin + rank, (8, here)).astype(BF)
    slots = jnp.dot(slots, row_tile_ref[...], preferred_element_type=F32)
    row_ref[...] = slots[:1].astype(jnp.int32) * TPS + token_ref[...]


def inverse_density(core, own, sib):
    rows = 2 * TILES * TPS
    row_tile = (np.arange(2 * TILES)[:, None] == np.arange(rows)[None, :] // TPS).astype(np.float32)
    token = np.tile(ROW_TOKEN, TILES)
    own_cell = (np.arange(CELLS)[:, None] % TPS == token[None, :]).astype(np.float32)
    tap = (np.arange(TAPS)[:, None] == np.arange(CELLS)[None, :] // TPS).astype(np.float32)
    vmem, smem = pl.BlockSpec(memory_space=pltpu.VMEM), pl.BlockSpec(memory_space=pltpu.SMEM)
    return pl.pallas_call(
        inverse_kernel,
        in_specs=[smem] + [vmem] * 6,
        out_shape=(jax.ShapeDtypeStruct((TAPS, rows), F32), jax.ShapeDtypeStruct((1, rows), jnp.int32)),
        compiler_params=pltpu.CompilerParams(vmem_limit_bytes=KERNEL_VMEM // 2),
        cost_estimate=SMALL,
        name="inverse_density",
    )(core, own, sib, jnp.asarray(token, jnp.int32)[None], *(jnp.asarray(v, BF) for v in (row_tile, own_cell, tap)))


def grid_kernel(swath_ref, pos_ref, center_ref, after_ref, out_ref, done_ref):
    channels = swath_ref.shape[1]
    gap = jnp.zeros((TAPS, 8, FP), F32)

    def step(tiles_ref):
        i = pl.program_id(0)
        blocks = []
        for pair in range(2):
            first, second = 4 * i + 2 * pair, 4 * i + 2 * pair + 1
            left = weights_at(pos_ref[first].astype(F32), center_ref, 0).reshape(TAPS, 16, FP)
            right = weights_at(pos_ref[second].astype(F32), center_ref, 2).reshape(TAPS, 16, FP)
            left = jnp.concatenate([left, gap], 1).reshape(TAPS * PAIR, FP)
            right = jnp.concatenate([gap, right], 1).reshape(TAPS * PAIR, FP)
            table = jnp.concatenate([left, right], 1).astype(BF)
            data = jnp.concatenate([tiles_ref[2 * pair], tiles_ref[2 * pair + 1]], 1)
            total = lax.dot_general(table, data, NT, preferred_element_type=F32)
            blocks.append(total.reshape(TAPS, PAIR, channels))
        base = pl.multiple_of(i * 2 * PAIR, 2 * PAIR)
        out_ref[:, pl.ds(base, 2 * PAIR), :] = jnp.concatenate(blocks, 1).astype(BF)

    pltpu.emit_pipeline(
        step, grid=(TILES // 4,), in_specs=[pl.BlockSpec((4, channels, FP), lambda i: (i, 0, 0))]
    )(swath_ref)
    done_ref[...] = after_ref[...]


def gridded(swath, pos, center, after):
    channels = swath.shape[1]
    vmem = pl.BlockSpec(memory_space=pltpu.VMEM)
    swath = pltpu.with_memory_space_constraint(swath, pltpu.HBM)
    return pl.pallas_call(
        grid_kernel,
        in_specs=[pl.BlockSpec(memory_space=pl.ANY), vmem, vmem, vmem],
        out_specs=(vmem, vmem),
        out_shape=(pltpu.VMEM((TAPS, TILES * TPS, channels), BF), jax.ShapeDtypeStruct((8, FP), F32)),
        compiler_params=pltpu.CompilerParams(vmem_limit_bytes=KERNEL_VMEM // 2),
        cost_estimate=SMALL,
        name="grid_tiles",
    )(swath, pos, center, after)


def embed_kernel(own_ref, sib_ref, *refs):
    *weight_refs, inverse_ref, column_ref, row_ref, out_ref, total, spread = refs
    channels = own_ref.shape[2]
    slot_rows, half = out_ref.shape[0], own_ref.shape[1]
    part = slot_rows // TAPS
    width = total.shape[1]
    total[...] = jnp.zeros_like(total)

    def tap(k, carry):
        weight = jnp.concatenate([w[:, k].reshape(-1, channels) for w in weight_refs], 0)
        scale = jnp.broadcast_to(inverse_ref[pl.ds(k, 1), :], (FP, 2 * half)).T
        scale = jnp.concatenate([scale] * (width // FP), 1)
        for n, ref in enumerate((own_ref, sib_ref)):
            rows = slice(n * half, (n + 1) * half)
            product = lax.dot_general(ref[k], weight, NT, preferred_element_type=F32)
            total[rows] += product * scale[rows]
        base = pl.multiple_of(k * part, part)
        here = lax.broadcasted_iota(jnp.int32, (part, 2 * half), 0) + base
        spread[pl.ds(base, part), :] = jnp.where(here == row_ref[...], 1.0, 0.0).astype(BF)
        return carry

    lax.fori_loop(0, TAPS, tap, 0, unroll=4)
    columns = lax.broadcasted_iota(jnp.int32, (width, width), 0)
    order = jnp.where(columns == column_ref[...], 1.0, 0.0).astype(BF)
    tokens = lax.dot_general(total[...].astype(BF), order, NT, preferred_element_type=F32).astype(BF)
    out_ref[...] = jnp.dot(spread[...], tokens, preferred_element_type=F32).astype(BF)


def embed(own, sib, weights, inverse, columns, rows):
    width = CHIPS * weights[0].shape[2]
    slot_rows = 2 * CHIPS * SLOTS * TPS
    half = TILES * TPS
    vmem = pl.BlockSpec(memory_space=pltpu.VMEM)
    large = [pltpu.with_memory_space_constraint(a, pltpu.VMEM) for a in (own, sib, *weights)]
    return pl.pallas_call(
        embed_kernel,
        in_specs=[vmem] * (len(large) + 3),
        out_specs=vmem,
        out_shape=jax.ShapeDtypeStruct((slot_rows, width), BF),
        scratch_shapes=[pltpu.VMEM((2 * half, width), F32), pltpu.VMEM((slot_rows, 2 * half), BF)],
        compiler_params=pltpu.CompilerParams(vmem_limit_bytes=KERNEL_VMEM // 2),
        cost_estimate=pl.CostEstimate(flops=2 * TAPS * 2 * half * 768 * width * 2, bytes_accessed=1000000, transcendentals=0),
        name="embed_tiles",
    )(*large, inverse, columns, rows)


def attend_kernel(tokens_ref, row_ref, bias_ref, gain_ref, kv_ref, latent_ref, out_ref):
    rows = TPS * PATCHES
    per_core = tokens_ref.shape[0] * tokens_ref.shape[2]
    width = 2 * tokens_ref.shape[3]
    hot = lax.broadcasted_iota(jnp.int32, (rows, per_core), 0) == row_ref[...]
    hot = jnp.where(hot, 1.0, 0.0).astype(BF)
    halves = [
        jnp.dot(hot, tokens_ref[:, c].reshape(per_core, width // 2), preferred_element_type=F32) for c in range(2)
    ]
    tokens = (jnp.concatenate(halves, 1) + bias_ref[...]).astype(BF).astype(F32)
    mean = jnp.mean(tokens, axis=1, keepdims=True)
    shifted = tokens - mean
    var = jnp.mean(shifted * shifted, axis=1, keepdims=True)
    normed = (shifted * lax.rsqrt(var + 1e-05) * gain_ref[...]).astype(BF)
    keys_values = jnp.dot(normed, kv_ref[...], preferred_element_type=F32).astype(BF)
    keys, values = keys_values[:, :width], keys_values[:, width:].astype(F32)
    head = lax.broadcasted_iota(jnp.int32, (HEADS, width), 0)
    lane_head = lax.shift_right_logical(lax.broadcasted_iota(jnp.int32, (HEADS, width), 1), int(math.log2(HD)))
    query = jnp.concatenate(
        [jnp.where(head == lane_head, jnp.broadcast_to(latent_ref[l : l + 1], (HEADS, width)), 0.0) for l in range(LEVELS)],
        0,
    )
    scores = jnp.zeros((rows, LEVELS * HEADS), F32)
    for _ in range(3):
        piece = query.astype(BF)
        scores += lax.dot_general(keys, piece, NT, preferred_element_type=F32)
        query = query - piece.astype(F32)
    scores = (scores * (1.0 / math.sqrt(HD))).reshape(TPS, PATCHES, LEVELS * HEADS)
    top = jnp.max(scores, axis=0)
    expo = jnp.exp(scores - top[None])
    mass = jnp.sum(expo, axis=0)
    expo = expo.reshape(rows, LEVELS * HEADS).astype(BF)
    values = values.reshape(TPS, PATCHES, width)
    parts = []
    for value, count in ((top, 3), (mass, 2)):
        for _ in range(count):
            piece = value.astype(BF)
            parts.append(piece)
            value = value - piece.astype(F32)
    pick = lax.broadcasted_iota(jnp.int32, (LEVELS * HEADS, width), 0)
    stat_row = lax.broadcasted_iota(jnp.int32, (LEVELS * HEADS, FP), 0)
    stat_lane = lax.broadcasted_iota(jnp.int32, (LEVELS * HEADS, FP), 1)
    lane = lax.shift_right_logical(lax.broadcasted_iota(jnp.int32, (LEVELS * HEADS, width), 1), int(math.log2(HD)))
    blocks = []
    for level in range(LEVELS):
        wide = jnp.where(pick == lane + level * HEADS, 1.0, 0.0).astype(BF)
        share = jnp.dot(expo, wide, preferred_element_type=F32).reshape(TPS, PATCHES, width)
        partial = jnp.sum(share * values, axis=0)
        stats = jnp.zeros((PATCHES, FP), F32)
        for n, piece in enumerate(parts):
            to = (stat_row - level * HEADS == stat_lane - n * HEADS) & (stat_row >= level * HEADS) & (stat_row < (level + 1) * HEADS)
            stats += jnp.dot(piece, jnp.where(to, 1.0, 0.0).astype(BF), preferred_element_type=F32)
        blocks.append(jnp.concatenate([partial, stats], 1).astype(BF))
    stacked = jnp.concatenate(blocks, 0)
    count = LEVELS * PATCHES
    target = lax.broadcasted_iota(jnp.int32, (count, count), 0)
    source = lax.broadcasted_iota(jnp.int32, (count, count), 1)
    moved = (target & (LEVELS - 1)) * PATCHES + lax.shift_right_logical(target, 2) == source
    out_ref[...] = jnp.dot(jnp.where(moved, 1.0, 0.0).astype(BF), stacked, preferred_element_type=F32).astype(BF)


def attend(tokens, rows, bias, gain, kv_weight, latents):
    width = kv_weight.shape[0]
    return pl.pallas_call(
        attend_kernel,
        out_shape=jax.ShapeDtypeStruct((PATCHES * LEVELS, width + FP), BF),
        compiler_params=pltpu.CompilerParams(vmem_limit_bytes=KERNEL_VMEM),
        cost_estimate=pl.CostEstimate(flops=2 * 384 * 512 * 4000, bytes_accessed=3000000, transcendentals=12288),
        name="attend_source",
    )(tokens, rows, bias, gain, kv_weight, latents)


def finish_kernel(parts_ref, weight_ref, out_ref):
    sources, rows, wide = parts_ref.shape
    width = wide - FP
    stats = parts_ref[:, :, width:].reshape(sources * rows, FP)
    row = lax.broadcasted_iota(jnp.int32, (FP, width), 0)
    head = lax.shift_right_logical(lax.broadcasted_iota(jnp.int32, (FP, width), 1), int(math.log2(HD)))
    same = (row & (HEADS - 1)) == head
    is_top = jnp.where(same & (row < 3 * HEADS), 1.0, 0.0).astype(BF)
    is_mass = jnp.where(same & (row >= 3 * HEADS) & (row < 5 * HEADS), 1.0, 0.0).astype(BF)
    top = jnp.dot(stats, is_top, preferred_element_type=F32).reshape(sources, rows, width)
    mass = jnp.dot(stats, is_mass, preferred_element_type=F32).reshape(sources, rows, width)
    scale = jnp.exp(top - jnp.max(top, axis=0)[None])
    above = jnp.sum(scale * parts_ref[:, :, :width].astype(F32), axis=0)
    attended = (above / jnp.sum(scale * mass, axis=0)).astype(BF)
    result = jnp.dot(attended, weight_ref[...], preferred_element_type=F32)
    for patch in range(rows // LEVELS):
        out_ref[patch] = result[patch * LEVELS : (patch + 1) * LEVELS]


def finish(parts, out_weight):
    return pl.pallas_call(
        finish_kernel,
        out_shape=jax.ShapeDtypeStruct((parts.shape[1] // LEVELS, LEVELS, out_weight.shape[1]), F32),
        cost_estimate=pl.CostEstimate(flops=2 * 128 * 128 * 1024, bytes_accessed=800000, transcendentals=65536),
        name="combine_sources",
    )(parts, out_weight)


def device_at(y, x, core):
    return ((y % SIDE) * SIDE + x % SIDE) * 2 + core


def shift(offset, second):
    pairs = []
    for y in range(SIDE):
        for x in range(SIDE):
            for core in range(2):
                along_x = (core == 0) != second
                to = device_at(y, x + offset, core) if along_x else device_at(y + offset, x, core)
                pairs.append((device_at(y, x, core), to))
    return pairs


def send(array, offset, second):
    return lax.ppermute(array, "lat", shift(offset, second))


def offset_at(index):
    return jnp.where(index == 0, 0, jnp.where(index == 1, -1, index - 1))


def index_of(offset):
    offset = offset % SIDE
    return jnp.where(offset == 0, 0, jnp.where(offset == SIDE - 1, 1, offset + 1))


def body(
    swath,
    tile_band,
    tile_patch,
    fp_pos,
    conv_weight,
    conv_bias,
    norm_gain,
    latents,
    kv_weight,
    out_weight,
):
    place = lax.axis_index("lat")
    core, chip = place % 2, place // 2
    chip_y, chip_x = chip // SIDE, chip % SIDE
    swath, fp_pos = swath[0], fp_pos[0]
    channels, cols = swath.shape[1], conv_weight.shape[4]
    width = kv_weight.shape[0]
    swap = [(i, i ^ 1) for i in range(2 * CHIPS)]

    shard = jnp.transpose(conv_weight[0].reshape(TAPS, channels, cols), (0, 2, 1))
    center = jnp.asarray(
        np.concatenate([centers(list(range(TPS)) + [-1] * 4), centers([-1] * 4 + list(ROW_TOKEN[TPS:]))], 0)
    )
    half = TAPS // 2
    up, down = send(shard, 1, False), send(shard, -1, False)
    sib_swath = lax.ppermute(swath, "lat", swap)
    sib_pos = lax.ppermute(fp_pos, "lat", swap)
    record = tile_records(tile_band[0, :, 0], tile_patch[0], fp_pos)
    up, down, record = lax.optimization_barrier((up, down, record))
    far = [send(up[:half], 1, False), send(down[half:], -1, False)]
    others = [send(record, -offset, False) for offset in OFFSETS[1:]]
    *far, record, sib_pos, swath = lax.optimization_barrier(
        (*far, jnp.stack([record] + others, 0), sib_pos, swath)
    )
    low = jnp.stack([shard, up], 0)
    high = jnp.stack([down, jnp.concatenate(far, 0)], 0)
    above_low, below_high = send(low, 1, True), send(high, -1, True)
    above_high, below_low = send(high, 1, True), send(low, -1, True)
    record = jnp.stack([record] + [send(record, -offset, True) for offset in OFFSETS[1:]], 0)
    own, after = gridded(swath, fp_pos, center, jnp.zeros((8, FP), F32))
    above_low, below_high, above_high, below_low, record, sib_swath, after = lax.optimization_barrier(
        (above_low, below_high, above_high, below_low, record, sib_swath, after)
    )
    corner_low, corner_high = send(above_low, 1, True), send(below_high, -1, True)
    sib_record = lax.ppermute(record, "lat", swap)
    sib, _ = gridded(sib_swath, sib_pos, center, after)
    weights = [low, high, above_low, above_high, below_low, below_high, corner_low, corner_high]

    inverse, rows = inverse_density(
        core[None].astype(jnp.int32), record.reshape(-1, RECORD), sib_record.reshape(-1, RECORD)
    )

    column = jnp.arange(CHIPS * cols, dtype=jnp.int32)[None, :]
    near, farther = offset_at(column // cols % SIDE), offset_at(column // cols // SIDE)
    at_y = (chip_y + jnp.where(core == 0, farther, near)) % SIDE
    at_x = (chip_x + jnp.where(core == 0, near, farther)) % SIDE
    columns = (at_y * SIDE + at_x) * cols + column % cols
    outgoing = embed(own, sib, weights, inverse, columns.astype(jnp.int32), rows)

    record, sib_record, conv_bias, norm_gain, kv_weight, outgoing = lax.optimization_barrier(
        (record, sib_record, conv_bias, norm_gain, kv_weight, outgoing)
    )
    about = jnp.stack([record[..., CELLS : CELLS + 2], sib_record[..., CELLS : CELLS + 2]])
    about = about.reshape(2, CHIPS, TILES, 2).astype(F32)
    outgoing = outgoing.reshape(2 * CHIPS, SLOTS * TPS, CHIPS * cols)
    incoming = lax.all_to_all(outgoing, "lat", split_axis=0, concat_axis=0, tiled=True)
    mine = about[..., 0] == place.astype(F32)
    patches = jnp.where(mine, about[..., 1] + 1, 0)
    before = jnp.einsum("cdt,tu->cdu", mine.astype(F32), jnp.asarray(np.triu(np.ones((TILES, TILES), np.float32), 1)))
    patch_at = jnp.stack([jnp.sum(jnp.where(before == n, patches, 0), axis=2) for n in range(2)], 2)
    number = jnp.arange(CHIPS)
    in_y, in_x = index_of(number // SIDE - chip_y), index_of(number % SIDE - chip_x)
    x_first, y_first = SIDE * in_y + in_x, SIDE * in_x + in_y
    order = jnp.stack([jnp.where(core == 0, x_first, y_first), jnp.where(core == 0, y_first, x_first)])
    hot = (order[:, :, None] == number[None, None, :]).astype(F32)
    patch_by = jnp.einsum("cnd,cdk->nck", hot, patch_at)
    patch_by = jnp.where(core == 0, patch_by, patch_by[:, ::-1])
    patch_in = patch_by.astype(jnp.int32).reshape(-1, 1) - 1
    token_in = jnp.where(patch_in < 0, -1, patch_in + PATCHES * jnp.arange(TPS)[None, :]).reshape(1, -1)

    def by_core(array):
        shape = array.shape[1:]
        split = array.reshape((CHIPS, 2, cols) + shape)
        return jnp.swapaxes(split, 0, 1).reshape((width,) + shape)

    parts = attend(
        incoming.reshape(CHIPS, 2, SLOTS * TPS, CHIPS * cols),
        token_in.astype(jnp.int32),
        by_core(conv_bias[0])[None],
        by_core(norm_gain)[None],
        by_core(kv_weight),
        latents,
    )
    sources = lax.axis_size("src")
    parts = lax.all_to_all(
        parts.reshape(sources, -1, width + FP), "src", split_axis=0, concat_axis=0, tiled=True
    )
    return finish(parts, out_weight)


def solution(mesh):
    in_specs = (
        P("src", "lat", None, None),
        P("src", "lat", None),
        P("src", "lat"),
        P("src", "lat", None, None),
        P("src", None, None, None, "lat"),
        P("src", None),
        P(),
        P(),
        P(),
        P(),
    )
    out_specs = P(("lat", "src"), None, None)
    return jax.shard_map(body, mesh=mesh, in_specs=in_specs, out_specs=out_specs, check_vma=False)
```

```python
import math

import jax
import jax.numpy as jnp
import numpy as np
from jax import lax
from jax.experimental import pallas as pl
from jax.experimental.pallas import tpu as pltpu
from jax.sharding import PartitionSpec as P

HEADS = 8
HD = 64
PW = 24
KS = 4
TPS = 12
LEVELS = 4
TILES = 32
PATCHES = 32
CHIPS = 16
SIDE = 4
CELLS = 192
TAPS = KS * KS
SLOTS = 4
FP = 128
PAIR = 2 * TPS
FAR = 1.0e4
OFFSETS = (0, -1, 1, 2)
ROW_TOKEN = np.array(list(range(TPS)) + [8, 9, 10, 11, 0, 1, 2, 3, 4, 5, 6, 7])
BF = jnp.bfloat16
F32 = jnp.float32
NT = (((1,), (1,)), ((), ()))
KERNEL_VMEM = 24 * 2**20
RECORD = 256
STEP = 16
SMALL = pl.CostEstimate(flops=1000000, bytes_accessed=10000, transcendentals=0)


def centers(tokens):
    rows, cols = [], []
    for tap in range(TAPS):
        for token in tokens:
            rows.append(token // 6 * KS + tap // KS + 0.5 if token >= 0 else FAR)
            cols.append(token % 6 * KS + tap % KS + 0.5 if token >= 0 else FAR)
    wide = [np.repeat(np.array(v, np.float32)[:, None], FP, 1) for v in (rows, cols)]
    return np.stack(wide)


def weights_at(pos, center_ref, index):
    down = pos[0:1] - center_ref[index]
    across = pos[1:2] - center_ref[index + 1]
    return jnp.exp((down * down + across * across) * (-1.0 / 1.125))


def record_kernel(band_ref, patch_ref, pos_ref, center_ref, out_ref):
    ones = jnp.ones((8, FP), BF)
    place = lax.broadcasted_iota(jnp.int32, (8, RECORD), 0)
    lane = lax.broadcasted_iota(jnp.int32, (8, RECORD - CELLS), 1)

    def group(g, carry):
        base = pl.multiple_of(g * 8, 8)
        total = jnp.zeros((8, RECORD), F32)
        for j in range(8):
            table = weights_at(pos_ref[base + j].astype(F32), center_ref, 0).astype(BF)
            row = lax.dot_general(ones, table, NT, preferred_element_type=F32)
            about = jnp.where(lane == 0, band_ref[base + j], patch_ref[base + j]).astype(F32)
            total = jnp.where(place == j, jnp.concatenate([row, about], 1), total)
        return carry + (total,)

    rows = ()
    for g in range(TILES // 8):
        rows = group(g, rows)
    out_ref[...] = jnp.concatenate(rows, 0).astype(BF)


def tile_records(band, patch, pos):
    vmem, smem = pl.BlockSpec(memory_space=pltpu.VMEM), pl.BlockSpec(memory_space=pltpu.SMEM)
    return pl.pallas_call(
        record_kernel,
        in_specs=[smem, smem, vmem, vmem],
        out_shape=jax.ShapeDtypeStruct((TILES, RECORD), BF),
        cost_estimate=SMALL,
        name="tile_records",
    )(band, patch, pos, jnp.asarray(centers(range(TPS))))


def inverse_kernel(core_ref, own_ref, sib_ref, token_ref, row_tile_ref, own_cell_ref, tap_ref, out_ref, row_ref):
    here = 2 * TILES

    def as_row(column):
        return jnp.broadcast_to(column, (column.shape[0], FP)).T[:1]

    about = jnp.concatenate([own_ref[:TILES, CELLS:], sib_ref[:TILES, CELLS:]], 0).astype(F32)
    band, target = about[:, :1], about[:, :1] * PATCHES + about[:, 1:2]
    band_row, target_row = as_row(band), as_row(target)
    total = jnp.ones((CELLS, here), F32)
    for ref in (own_ref, sib_ref):
        about = ref[:, CELLS:].astype(F32)
        same = jnp.where(about[:, :1] * PATCHES + about[:, 1:2] == target_row, 1.0, 0.0).astype(BF)
        total += lax.dot_general(ref[:, :CELLS], same, (((0,), (0,)), ((), ())), preferred_element_type=F32)
    inverse = 1.0 / total
    out = jnp.zeros(out_ref.shape, F32)
    for _ in range(3):
        piece = inverse.astype(BF)
        spread = jnp.dot(piece, row_tile_ref[...], preferred_element_type=F32).astype(BF) * own_cell_ref[...]
        out += jnp.dot(tap_ref[...], spread, preferred_element_type=F32)
        inverse = inverse - piece.astype(F32)
    out_ref[...] = out
    other = lax.broadcasted_iota(jnp.int32, (here, here), 0)
    tile = lax.broadcasted_iota(jnp.int32, (here, here), 1)
    earlier = (other < tile) & ((other < TILES) == (tile < TILES)) & (band == band_row)
    rank = jnp.sum(jnp.where(earlier, 1.0, 0.0), axis=0, keepdims=True)
    origin = jnp.where(tile[:1] < TILES, core_ref[0], 1 - core_ref[0]).astype(F32)
    slots = jnp.broadcast_to(band_row * SLOTS + 2 * origin + rank, (8, here)).astype(BF)
    slots = jnp.dot(slots, row_tile_ref[...], preferred_element_type=F32)
    row_ref[...] = slots[:1].astype(jnp.int32) * TPS + token_ref[...]


def inverse_density(core, own, sib):
    rows = 2 * TILES * TPS
    row_tile = (np.arange(2 * TILES)[:, None] == np.arange(rows)[None, :] // TPS).astype(np.float32)
    token = np.tile(ROW_TOKEN, TILES)
    own_cell = (np.arange(CELLS)[:, None] % TPS == token[None, :]).astype(np.float32)
    tap = (np.arange(TAPS)[:, None] == np.arange(CELLS)[None, :] // TPS).astype(np.float32)
    vmem, smem = pl.BlockSpec(memory_space=pltpu.VMEM), pl.BlockSpec(memory_space=pltpu.SMEM)
    return pl.pallas_call(
        inverse_kernel,
        in_specs=[smem] + [vmem] * 6,
        out_shape=(jax.ShapeDtypeStruct((TAPS, rows), F32), jax.ShapeDtypeStruct((1, rows), jnp.int32)),
        compiler_params=pltpu.CompilerParams(vmem_limit_bytes=KERNEL_VMEM // 2),
        cost_estimate=SMALL,
        name="inverse_density",
    )(core, own, sib, jnp.asarray(token, jnp.int32)[None], *(jnp.asarray(v, BF) for v in (row_tile, own_cell, tap)))


def grid_kernel(swath_ref, pos_ref, center_ref, out_ref):
    channels = swath_ref.shape[1]
    gap = jnp.zeros((TAPS, 8, FP), F32)

    def step(tiles_ref):
        i = pl.program_id(0)
        for quad in range(STEP // 4):
            blocks = []
            for pair in range(2):
                place = 4 * quad + 2 * pair
                first, second = STEP * i + place, STEP * i + place + 1
                left = weights_at(pos_ref[first].astype(F32), center_ref, 0).reshape(TAPS, 16, FP)
                right = weights_at(pos_ref[second].astype(F32), center_ref, 2).reshape(TAPS, 16, FP)
                left = jnp.concatenate([left, gap], 1).reshape(TAPS * PAIR, FP)
                right = jnp.concatenate([gap, right], 1).reshape(TAPS * PAIR, FP)
                table = jnp.concatenate([left, right], 1).astype(BF)
                data = jnp.concatenate([tiles_ref[place], tiles_ref[place + 1]], 1)
                total = lax.dot_general(table, data, NT, preferred_element_type=F32)
                blocks.append(total.reshape(TAPS, PAIR, channels))
            base = pl.multiple_of((STEP // 4 * i + quad) * 2 * PAIR, 2 * PAIR)
            out_ref[:, pl.ds(base, 2 * PAIR), :] = jnp.concatenate(blocks, 1).astype(BF)

    pltpu.emit_pipeline(
        step, grid=(TILES // STEP,), in_specs=[pl.BlockSpec((STEP, channels, FP), lambda i: (i, 0, 0))]
    )(swath_ref)


def gridded(swath, pos, center):
    channels = swath.shape[1]
    vmem = pl.BlockSpec(memory_space=pltpu.VMEM)
    swath = pltpu.with_memory_space_constraint(swath, pltpu.HBM)
    return pl.pallas_call(
        grid_kernel,
        in_specs=[pl.BlockSpec(memory_space=pl.ANY), vmem, vmem],
        out_specs=vmem,
        out_shape=pltpu.VMEM((TAPS, TILES * TPS, channels), BF),
        compiler_params=pltpu.CompilerParams(vmem_limit_bytes=KERNEL_VMEM // 2),
        cost_estimate=SMALL,
        name="grid_tiles",
    )(swath, pos, center)


def embed_kernel(own_ref, sib_ref, *refs):
    *weight_refs, inverse_ref, column_ref, row_ref, out_ref, total, spread = refs
    channels = own_ref.shape[2]
    slot_rows, half = out_ref.shape[0], own_ref.shape[1]
    part = slot_rows // TAPS
    width = total.shape[1]
    total[...] = jnp.zeros_like(total)

    def tap(k, carry):
        weight = jnp.concatenate([w[:, k].reshape(-1, channels) for w in weight_refs], 0)
        scale = jnp.broadcast_to(inverse_ref[pl.ds(k, 1), :], (FP, 2 * half)).T
        scale = jnp.concatenate([scale] * (width // FP), 1)
        for n, ref in enumerate((own_ref, sib_ref)):
            rows = slice(n * half, (n + 1) * half)
            product = lax.dot_general(ref[k], weight, NT, preferred_element_type=F32)
            total[rows] += product * scale[rows]
        base = pl.multiple_of(k * part, part)
        here = lax.broadcasted_iota(jnp.int32, (part, 2 * half), 0) + base
        spread[pl.ds(base, part), :] = jnp.where(here == row_ref[...], 1.0, 0.0).astype(BF)
        return carry

    lax.fori_loop(0, TAPS, tap, 0, unroll=8)
    columns = lax.broadcasted_iota(jnp.int32, (width, width), 0)
    order = jnp.where(columns == column_ref[...], 1.0, 0.0).astype(BF)
    tokens = lax.dot_general(total[...].astype(BF), order, NT, preferred_element_type=F32).astype(BF)
    out_ref[...] = jnp.dot(spread[...], tokens, preferred_element_type=F32).astype(BF)


def embed(own, sib, weights, inverse, columns, rows):
    width = CHIPS * weights[0].shape[2]
    slot_rows = 2 * CHIPS * SLOTS * TPS
    half = TILES * TPS
    vmem = pl.BlockSpec(memory_space=pltpu.VMEM)
    large = [pltpu.with_memory_space_constraint(a, pltpu.VMEM) for a in (own, sib, *weights)]
    return pl.pallas_call(
        embed_kernel,
        in_specs=[vmem] * (len(large) + 3),
        out_specs=vmem,
        out_shape=jax.ShapeDtypeStruct((slot_rows, width), BF),
        scratch_shapes=[pltpu.VMEM((2 * half, width), F32), pltpu.VMEM((slot_rows, 2 * half), BF)],
        compiler_params=pltpu.CompilerParams(vmem_limit_bytes=KERNEL_VMEM // 2),
        cost_estimate=pl.CostEstimate(flops=2 * TAPS * 2 * half * 768 * width * 2, bytes_accessed=1000000, transcendentals=0),
        name="embed_tiles",
    )(*large, inverse, columns, rows)


def attend_kernel(tokens_ref, row_ref, bias_ref, gain_ref, kv_ref, latent_ref, out_ref):
    rows = TPS * PATCHES
    per_core = tokens_ref.shape[0] * tokens_ref.shape[2]
    width = 2 * tokens_ref.shape[3]
    hot = lax.broadcasted_iota(jnp.int32, (rows, per_core), 0) == row_ref[...]
    hot = jnp.where(hot, 1.0, 0.0).astype(BF)
    halves = [
        jnp.dot(hot, tokens_ref[:, c].reshape(per_core, width // 2), preferred_element_type=F32) for c in range(2)
    ]
    tokens = (jnp.concatenate(halves, 1) + bias_ref[...]).astype(BF).astype(F32)
    mean = jnp.mean(tokens, axis=1, keepdims=True)
    shifted = tokens - mean
    var = jnp.mean(shifted * shifted, axis=1, keepdims=True)
    normed = (shifted * lax.rsqrt(var + 1e-05) * gain_ref[...]).astype(BF)
    keys_values = jnp.dot(normed, kv_ref[...], preferred_element_type=F32).astype(BF)
    keys, values = keys_values[:, :width], keys_values[:, width:].astype(F32)
    head = lax.broadcasted_iota(jnp.int32, (HEADS, width), 0)
    lane_head = lax.shift_right_logical(lax.broadcasted_iota(jnp.int32, (HEADS, width), 1), int(math.log2(HD)))
    query = jnp.concatenate(
        [jnp.where(head == lane_head, jnp.broadcast_to(latent_ref[l : l + 1], (HEADS, width)), 0.0) for l in range(LEVELS)],
        0,
    )
    scores = jnp.zeros((rows, LEVELS * HEADS), F32)
    for _ in range(3):
        piece = query.astype(BF)
        scores += lax.dot_general(keys, piece, NT, preferred_element_type=F32)
        query = query - piece.astype(F32)
    scores = (scores * (1.0 / math.sqrt(HD))).reshape(TPS, PATCHES, LEVELS * HEADS)
    top = jnp.max(scores, axis=0)
    expo = jnp.exp(scores - top[None])
    mass = jnp.sum(expo, axis=0)
    expo = expo.reshape(rows, LEVELS * HEADS).astype(BF)
    values = values.reshape(TPS, PATCHES, width)
    parts = []
    for value, count in ((top, 3), (mass, 2)):
        for _ in range(count):
            piece = value.astype(BF)
            parts.append(piece)
            value = value - piece.astype(F32)
    pick = lax.broadcasted_iota(jnp.int32, (LEVELS * HEADS, width), 0)
    stat_row = lax.broadcasted_iota(jnp.int32, (LEVELS * HEADS, FP), 0)
    stat_lane = lax.broadcasted_iota(jnp.int32, (LEVELS * HEADS, FP), 1)
    lane = lax.shift_right_logical(lax.broadcasted_iota(jnp.int32, (LEVELS * HEADS, width), 1), int(math.log2(HD)))
    blocks = []
    for level in range(LEVELS):
        wide = jnp.where(pick == lane + level * HEADS, 1.0, 0.0).astype(BF)
        share = jnp.dot(expo, wide, preferred_element_type=F32).reshape(TPS, PATCHES, width)
        partial = jnp.sum(share * values, axis=0)
        stats = jnp.zeros((PATCHES, FP), F32)
        for n, piece in enumerate(parts):
            to = (stat_row - level * HEADS == stat_lane - n * HEADS) & (stat_row >= level * HEADS) & (stat_row < (level + 1) * HEADS)
            stats += jnp.dot(piece, jnp.where(to, 1.0, 0.0).astype(BF), preferred_element_type=F32)
        blocks.append(jnp.concatenate([partial, stats], 1).astype(BF))
    stacked = jnp.concatenate(blocks, 0)
    count = LEVELS * PATCHES
    target = lax.broadcasted_iota(jnp.int32, (count, count), 0)
    source = lax.broadcasted_iota(jnp.int32, (count, count), 1)
    moved = (target & (LEVELS - 1)) * PATCHES + lax.shift_right_logical(target, 2) == source
    out_ref[...] = jnp.dot(jnp.where(moved, 1.0, 0.0).astype(BF), stacked, preferred_element_type=F32).astype(BF)


def attend(tokens, rows, bias, gain, kv_weight, latents):
    width = kv_weight.shape[0]
    return pl.pallas_call(
        attend_kernel,
        out_shape=jax.ShapeDtypeStruct((PATCHES * LEVELS, width + FP), BF),
        compiler_params=pltpu.CompilerParams(vmem_limit_bytes=KERNEL_VMEM),
        cost_estimate=pl.CostEstimate(flops=2 * 384 * 512 * 4000, bytes_accessed=3000000, transcendentals=12288),
        name="attend_source",
    )(tokens, rows, bias, gain, kv_weight, latents)


def finish_kernel(parts_ref, weight_ref, out_ref):
    sources, rows, wide = parts_ref.shape
    width = wide - FP
    stats = parts_ref[:, :, width:].reshape(sources * rows, FP)
    row = lax.broadcasted_iota(jnp.int32, (FP, width), 0)
    head = lax.shift_right_logical(lax.broadcasted_iota(jnp.int32, (FP, width), 1), int(math.log2(HD)))
    same = (row & (HEADS - 1)) == head
    is_top = jnp.where(same & (row < 3 * HEADS), 1.0, 0.0).astype(BF)
    is_mass = jnp.where(same & (row >= 3 * HEADS) & (row < 5 * HEADS), 1.0, 0.0).astype(BF)
    top = jnp.dot(stats, is_top, preferred_element_type=F32).reshape(sources, rows, width)
    mass = jnp.dot(stats, is_mass, preferred_element_type=F32).reshape(sources, rows, width)
    scale = jnp.exp(top - jnp.max(top, axis=0)[None])
    above = jnp.sum(scale * parts_ref[:, :, :width].astype(F32), axis=0)
    attended = (above / jnp.sum(scale * mass, axis=0)).astype(BF)
    result = jnp.dot(attended, weight_ref[...], preferred_element_type=F32)
    for patch in range(rows // LEVELS):
        out_ref[patch] = result[patch * LEVELS : (patch + 1) * LEVELS]


def finish(parts, out_weight):
    return pl.pallas_call(
        finish_kernel,
        out_shape=jax.ShapeDtypeStruct((parts.shape[1] // LEVELS, LEVELS, out_weight.shape[1]), F32),
        cost_estimate=pl.CostEstimate(flops=2 * 128 * 128 * 1024, bytes_accessed=800000, transcendentals=65536),
        name="combine_sources",
    )(parts, out_weight)


def device_at(y, x, core):
    return ((y % SIDE) * SIDE + x % SIDE) * 2 + core


def shift(offset, second):
    pairs = []
    for y in range(SIDE):
        for x in range(SIDE):
            for core in range(2):
                along_x = (core == 0) != second
                to = device_at(y, x + offset, core) if along_x else device_at(y + offset, x, core)
                pairs.append((device_at(y, x, core), to))
    return pairs


def send(array, offset, second):
    return lax.ppermute(array, "lat", shift(offset, second))


def offset_at(index):
    return jnp.where(index == 0, 0, jnp.where(index == 1, -1, index - 1))


def index_of(offset):
    offset = offset % SIDE
    return jnp.where(offset == 0, 0, jnp.where(offset == SIDE - 1, 1, offset + 1))


def body(
    swath,
    tile_band,
    tile_patch,
    fp_pos,
    conv_weight,
    conv_bias,
    norm_gain,
    latents,
    kv_weight,
    out_weight,
):
    place = lax.axis_index("lat")
    core, chip = place % 2, place // 2
    chip_y, chip_x = chip // SIDE, chip % SIDE
    swath, fp_pos = swath[0], fp_pos[0]
    channels, cols = swath.shape[1], conv_weight.shape[4]
    width = kv_weight.shape[0]
    swap = [(i, i ^ 1) for i in range(2 * CHIPS)]

    shard = jnp.transpose(conv_weight[0].reshape(TAPS, channels, cols), (0, 2, 1))
    center = jnp.asarray(
        np.concatenate([centers(list(range(TPS)) + [-1] * 4), centers([-1] * 4 + list(ROW_TOKEN[TPS:]))], 0)
    )
    half = TAPS // 2
    up, down = send(shard, 1, False), send(shard, -1, False)
    sib_swath = lax.ppermute(swath, "lat", swap)
    sib_pos = lax.ppermute(fp_pos, "lat", swap)
    record = tile_records(tile_band[0, :, 0], tile_patch[0], fp_pos)
    up, down, record = lax.optimization_barrier((up, down, record))
    far = [send(up[:half], 1, False), send(down[half:], -1, False)]
    others = [send(record, -offset, False) for offset in OFFSETS[1:]]
    *far, record, sib_pos = lax.optimization_barrier((*far, jnp.stack([record] + others, 0), sib_pos))
    low = jnp.stack([shard, up], 0)
    high = jnp.stack([down, jnp.concatenate(far, 0)], 0)
    above_low, below_high = send(low, 1, True), send(high, -1, True)
    record = jnp.stack([record] + [send(record, -offset, True) for offset in OFFSETS[1:]], 0)
    above_low, below_high, low, high, record, swath, sib_swath = lax.optimization_barrier(
        (above_low, below_high, low, high, record, swath, sib_swath)
    )
    corner_low, corner_high = send(above_low, 1, True), send(below_high, -1, True)
    above_high, below_low = send(high, 1, True), send(low, -1, True)
    sib_record = lax.ppermute(record, "lat", swap)
    own = gridded(swath, fp_pos, center)
    sib = gridded(sib_swath, sib_pos, center)
    weights = [low, high, above_low, above_high, below_low, below_high, corner_low, corner_high]

    inverse, rows = inverse_density(
        core[None].astype(jnp.int32), record.reshape(-1, RECORD), sib_record.reshape(-1, RECORD)
    )

    column = jnp.arange(CHIPS * cols, dtype=jnp.int32)[None, :]
    near, farther = offset_at(column // cols % SIDE), offset_at(column // cols // SIDE)
    at_y = (chip_y + jnp.where(core == 0, farther, near)) % SIDE
    at_x = (chip_x + jnp.where(core == 0, near, farther)) % SIDE
    columns = (at_y * SIDE + at_x) * cols + column % cols
    outgoing = embed(own, sib, weights, inverse, columns.astype(jnp.int32), rows)

    record, sib_record, conv_bias, norm_gain, kv_weight, outgoing = lax.optimization_barrier(
        (record, sib_record, conv_bias, norm_gain, kv_weight, outgoing)
    )
    about = jnp.stack([record[..., CELLS : CELLS + 2], sib_record[..., CELLS : CELLS + 2]])
    about = about.reshape(2, CHIPS, TILES, 2).astype(F32)
    outgoing = outgoing.reshape(2 * CHIPS, SLOTS * TPS, CHIPS * cols)
    incoming = lax.all_to_all(outgoing, "lat", split_axis=0, concat_axis=0, tiled=True)
    mine = about[..., 0] == place.astype(F32)
    patches = jnp.where(mine, about[..., 1] + 1, 0)
    before = jnp.einsum("cdt,tu->cdu", mine.astype(F32), jnp.asarray(np.triu(np.ones((TILES, TILES), np.float32), 1)))
    patch_at = jnp.stack([jnp.sum(jnp.where(before == n, patches, 0), axis=2) for n in range(2)], 2)
    number = jnp.arange(CHIPS)
    in_y, in_x = index_of(number // SIDE - chip_y), index_of(number % SIDE - chip_x)
    x_first, y_first = SIDE * in_y + in_x, SIDE * in_x + in_y
    order = jnp.stack([jnp.where(core == 0, x_first, y_first), jnp.where(core == 0, y_first, x_first)])
    hot = (order[:, :, None] == number[None, None, :]).astype(F32)
    patch_by = jnp.einsum("cnd,cdk->nck", hot, patch_at)
    patch_by = jnp.where(core == 0, patch_by, patch_by[:, ::-1])
    patch_in = patch_by.astype(jnp.int32).reshape(-1, 1) - 1
    token_in = jnp.where(patch_in < 0, -1, patch_in + PATCHES * jnp.arange(TPS)[None, :]).reshape(1, -1)

    def by_core(array):
        shape = array.shape[1:]
        split = array.reshape((CHIPS, 2, cols) + shape)
        return jnp.swapaxes(split, 0, 1).reshape((width,) + shape)

    parts = attend(
        incoming.reshape(CHIPS, 2, SLOTS * TPS, CHIPS * cols),
        token_in.astype(jnp.int32),
        by_core(conv_bias[0])[None],
        by_core(norm_gain)[None],
        by_core(kv_weight),
        latents,
    )
    sources = lax.axis_size("src")
    parts = lax.all_to_all(
        parts.reshape(sources, -1, width + FP), "src", split_axis=0, concat_axis=0, tiled=True
    )
    return finish(parts, out_weight)


def solution(mesh):
    in_specs = (
        P("src", "lat", None, None),
        P("src", "lat", None),
        P("src", "lat"),
        P("src", "lat", None, None),
        P("src", None, None, None, "lat"),
        P("src", None),
        P(),
        P(),
        P(),
        P(),
    )
    out_specs = P(("lat", "src"), None, None)
    return jax.shard_map(body, mesh=mesh, in_specs=in_specs, out_specs=out_specs, check_vma=False)
```

```python
import math

import jax
import jax.numpy as jnp
import numpy as np
from jax import lax
from jax.experimental import pallas as pl
from jax.experimental.pallas import tpu as pltpu
from jax.sharding import PartitionSpec as P

HEADS = 8
HD = 64
PW = 24
KS = 4
TPS = 12
LEVELS = 4
TILES = 32
PATCHES = 32
CHIPS = 16
SIDE = 4
CELLS = 192
TAPS = KS * KS
SLOTS = 4
FP = 128
PAIR = 2 * TPS
FAR = 1.0e4
OFFSETS = (0, -1, 1, 2)
ROW_TOKEN = np.array(list(range(TPS)) + [8, 9, 10, 11, 0, 1, 2, 3, 4, 5, 6, 7])
BF = jnp.bfloat16
F32 = jnp.float32
NT = (((1,), (1,)), ((), ()))
KERNEL_VMEM = 24 * 2**20
RECORD = 256
STEP = 16
SMALL = pl.CostEstimate(flops=1000000, bytes_accessed=10000, transcendentals=0)


def centers(tokens):
    rows, cols = [], []
    for tap in range(TAPS):
        for token in tokens:
            rows.append(token // 6 * KS + tap // KS + 0.5 if token >= 0 else FAR)
            cols.append(token % 6 * KS + tap % KS + 0.5 if token >= 0 else FAR)
    wide = [np.repeat(np.array(v, np.float32)[:, None], FP, 1) for v in (rows, cols)]
    return np.stack(wide)


def weights_at(pos, center_ref, index):
    down = pos[0:1] - center_ref[index]
    across = pos[1:2] - center_ref[index + 1]
    return jnp.exp((down * down + across * across) * (-1.0 / 1.125))


def record_kernel(band_ref, patch_ref, pos_ref, center_ref, out_ref):
    ones = jnp.ones((8, FP), BF)
    place = lax.broadcasted_iota(jnp.int32, (8, RECORD), 0)
    lane = lax.broadcasted_iota(jnp.int32, (8, RECORD - CELLS), 1)

    def group(g, carry):
        base = pl.multiple_of(g * 8, 8)
        total = jnp.zeros((8, RECORD), F32)
        for j in range(8):
            table = weights_at(pos_ref[base + j].astype(F32), center_ref, 0).astype(BF)
            row = lax.dot_general(ones, table, NT, preferred_element_type=F32)
            about = jnp.where(lane == 0, band_ref[base + j], patch_ref[base + j]).astype(F32)
            total = jnp.where(place == j, jnp.concatenate([row, about], 1), total)
        return carry + (total,)

    rows = ()
    for g in range(TILES // 8):
        rows = group(g, rows)
    out_ref[...] = jnp.concatenate(rows, 0).astype(BF)


def tile_records(band, patch, pos):
    vmem, smem = pl.BlockSpec(memory_space=pltpu.VMEM), pl.BlockSpec(memory_space=pltpu.SMEM)
    return pl.pallas_call(
        record_kernel,
        in_specs=[smem, smem, vmem, vmem],
        out_shape=jax.ShapeDtypeStruct((TILES, RECORD), BF),
        cost_estimate=SMALL,
        name="tile_records",
    )(band, patch, pos, jnp.asarray(centers(range(TPS))))


def inverse_kernel(core_ref, own_ref, sib_ref, token_ref, row_tile_ref, own_cell_ref, tap_ref, out_ref, row_ref):
    here = 2 * TILES

    def as_row(column):
        return jnp.broadcast_to(column, (column.shape[0], FP)).T[:1]

    about = jnp.concatenate([own_ref[:TILES, CELLS:], sib_ref[:TILES, CELLS:]], 0).astype(F32)
    band, target = about[:, :1], about[:, :1] * PATCHES + about[:, 1:2]
    band_row, target_row = as_row(band), as_row(target)
    total = jnp.ones((CELLS, here), F32)
    for ref in (own_ref, sib_ref):
        about = ref[:, CELLS:].astype(F32)
        same = jnp.where(about[:, :1] * PATCHES + about[:, 1:2] == target_row, 1.0, 0.0).astype(BF)
        total += lax.dot_general(ref[:, :CELLS], same, (((0,), (0,)), ((), ())), preferred_element_type=F32)
    inverse = 1.0 / total
    out = jnp.zeros(out_ref.shape, F32)
    for _ in range(3):
        piece = inverse.astype(BF)
        spread = jnp.dot(piece, row_tile_ref[...], preferred_element_type=F32).astype(BF) * own_cell_ref[...]
        out += jnp.dot(tap_ref[...], spread, preferred_element_type=F32)
        inverse = inverse - piece.astype(F32)
    out_ref[...] = out
    other = lax.broadcasted_iota(jnp.int32, (here, here), 0)
    tile = lax.broadcasted_iota(jnp.int32, (here, here), 1)
    earlier = (other < tile) & ((other < TILES) == (tile < TILES)) & (band == band_row)
    rank = jnp.sum(jnp.where(earlier, 1.0, 0.0), axis=0, keepdims=True)
    origin = jnp.where(tile[:1] < TILES, core_ref[0], 1 - core_ref[0]).astype(F32)
    slots = jnp.broadcast_to(band_row * SLOTS + 2 * origin + rank, (8, here)).astype(BF)
    slots = jnp.dot(slots, row_tile_ref[...], preferred_element_type=F32)
    row_ref[...] = slots[:1].astype(jnp.int32) * TPS + token_ref[...]


def inverse_density(core, own, sib):
    rows = 2 * TILES * TPS
    row_tile = (np.arange(2 * TILES)[:, None] == np.arange(rows)[None, :] // TPS).astype(np.float32)
    token = np.tile(ROW_TOKEN, TILES)
    own_cell = (np.arange(CELLS)[:, None] % TPS == token[None, :]).astype(np.float32)
    tap = (np.arange(TAPS)[:, None] == np.arange(CELLS)[None, :] // TPS).astype(np.float32)
    vmem, smem = pl.BlockSpec(memory_space=pltpu.VMEM), pl.BlockSpec(memory_space=pltpu.SMEM)
    return pl.pallas_call(
        inverse_kernel,
        in_specs=[smem] + [vmem] * 6,
        out_shape=(jax.ShapeDtypeStruct((TAPS, rows), F32), jax.ShapeDtypeStruct((1, rows), jnp.int32)),
        compiler_params=pltpu.CompilerParams(vmem_limit_bytes=KERNEL_VMEM // 2),
        cost_estimate=SMALL,
        name="inverse_density",
    )(core, own, sib, jnp.asarray(token, jnp.int32)[None], *(jnp.asarray(v, BF) for v in (row_tile, own_cell, tap)))


def grid_kernel(swath_ref, pos_ref, center_ref, out_ref):
    channels = swath_ref.shape[1]
    gap = jnp.zeros((TAPS, 8, FP), F32)

    def step(tiles_ref):
        i = pl.program_id(0)
        for quad in range(STEP // 4):
            blocks = []
            for pair in range(2):
                place = 4 * quad + 2 * pair
                first, second = STEP * i + place, STEP * i + place + 1
                left = weights_at(pos_ref[first].astype(F32), center_ref, 0).reshape(TAPS, 16, FP)
                right = weights_at(pos_ref[second].astype(F32), center_ref, 2).reshape(TAPS, 16, FP)
                left = jnp.concatenate([left, gap], 1).reshape(TAPS * PAIR, FP)
                right = jnp.concatenate([gap, right], 1).reshape(TAPS * PAIR, FP)
                table = jnp.concatenate([left, right], 1).astype(BF)
                data = jnp.concatenate([tiles_ref[place], tiles_ref[place + 1]], 1)
                total = lax.dot_general(table, data, NT, preferred_element_type=F32)
                blocks.append(total.reshape(TAPS, PAIR, channels))
            base = pl.multiple_of((STEP // 4 * i + quad) * 2 * PAIR, 2 * PAIR)
            out_ref[:, pl.ds(base, 2 * PAIR), :] = jnp.concatenate(blocks, 1).astype(BF)

    pltpu.emit_pipeline(
        step, grid=(TILES // STEP,), in_specs=[pl.BlockSpec((STEP, channels, FP), lambda i: (i, 0, 0))]
    )(swath_ref)


def gridded(swath, pos, center):
    channels = swath.shape[1]
    vmem = pl.BlockSpec(memory_space=pltpu.VMEM)
    swath = pltpu.with_memory_space_constraint(swath, pltpu.HBM)
    return pl.pallas_call(
        grid_kernel,
        in_specs=[pl.BlockSpec(memory_space=pl.ANY), vmem, vmem],
        out_specs=vmem,
        out_shape=pltpu.VMEM((TAPS, TILES * TPS, channels), BF),
        compiler_params=pltpu.CompilerParams(vmem_limit_bytes=KERNEL_VMEM // 2),
        cost_estimate=SMALL,
        name="grid_tiles",
    )(swath, pos, center)


def embed_kernel(own_ref, sib_ref, *refs):
    *weight_refs, inverse_ref, column_ref, row_ref, out_ref, total, spread = refs
    channels = own_ref.shape[2]
    slot_rows, half = out_ref.shape[0], own_ref.shape[1]
    part = slot_rows // TAPS
    width = total.shape[1]
    total[...] = jnp.zeros_like(total)

    def tap(k, carry):
        weight = jnp.concatenate([w[:, k].reshape(-1, channels) for w in weight_refs], 0)
        scale = jnp.broadcast_to(inverse_ref[pl.ds(k, 1), :], (FP, 2 * half)).T
        scale = jnp.concatenate([scale] * (width // FP), 1)
        for n, ref in enumerate((own_ref, sib_ref)):
            rows = slice(n * half, (n + 1) * half)
            product = lax.dot_general(ref[k], weight, NT, preferred_element_type=F32)
            total[rows] += product * scale[rows]
        base = pl.multiple_of(k * part, part)
        here = lax.broadcasted_iota(jnp.int32, (part, 2 * half), 0) + base
        spread[pl.ds(base, part), :] = jnp.where(here == row_ref[...], 1.0, 0.0).astype(BF)
        return carry

    lax.fori_loop(0, TAPS, tap, 0, unroll=8)
    columns = lax.broadcasted_iota(jnp.int32, (width, width), 0)
    order = jnp.where(columns == column_ref[...], 1.0, 0.0).astype(BF)
    tokens = lax.dot_general(total[...].astype(BF), order, NT, preferred_element_type=F32).astype(BF)
    out_ref[...] = jnp.dot(spread[...], tokens, preferred_element_type=F32).astype(BF)


def embed(own, sib, weights, inverse, columns, rows):
    width = CHIPS * weights[0].shape[2]
    slot_rows = 2 * CHIPS * SLOTS * TPS
    half = TILES * TPS
    vmem = pl.BlockSpec(memory_space=pltpu.VMEM)
    large = [pltpu.with_memory_space_constraint(a, pltpu.VMEM) for a in (own, sib, *weights)]
    return pl.pallas_call(
        embed_kernel,
        in_specs=[vmem] * (len(large) + 3),
        out_specs=vmem,
        out_shape=jax.ShapeDtypeStruct((slot_rows, width), BF),
        scratch_shapes=[pltpu.VMEM((2 * half, width), F32), pltpu.VMEM((slot_rows, 2 * half), BF)],
        compiler_params=pltpu.CompilerParams(vmem_limit_bytes=KERNEL_VMEM // 2),
        cost_estimate=pl.CostEstimate(flops=2 * TAPS * 2 * half * 768 * width * 2, bytes_accessed=1000000, transcendentals=0),
        name="embed_tiles",
    )(*large, inverse, columns, rows)


def attend_kernel(tokens_ref, row_ref, bias_ref, gain_ref, kv_ref, latent_ref, out_ref):
    rows = TPS * PATCHES
    per_core = tokens_ref.shape[0] * tokens_ref.shape[2]
    width = 2 * tokens_ref.shape[3]
    hot = lax.broadcasted_iota(jnp.int32, (rows, per_core), 0) == row_ref[...]
    hot = jnp.where(hot, 1.0, 0.0).astype(BF)
    halves = [
        jnp.dot(hot, tokens_ref[:, c].reshape(per_core, width // 2), preferred_element_type=F32) for c in range(2)
    ]
    tokens = (jnp.concatenate(halves, 1) + bias_ref[...]).astype(BF).astype(F32)
    mean = jnp.mean(tokens, axis=1, keepdims=True)
    shifted = tokens - mean
    var = jnp.mean(shifted * shifted, axis=1, keepdims=True)
    normed = (shifted * lax.rsqrt(var + 1e-05) * gain_ref[...]).astype(BF)
    keys_values = jnp.dot(normed, kv_ref[...], preferred_element_type=F32).astype(BF)
    keys, values = keys_values[:, :width], keys_values[:, width:].astype(F32)
    head = lax.broadcasted_iota(jnp.int32, (HEADS, width), 0)
    lane_head = lax.shift_right_logical(lax.broadcasted_iota(jnp.int32, (HEADS, width), 1), int(math.log2(HD)))
    query = jnp.concatenate(
        [jnp.where(head == lane_head, jnp.broadcast_to(latent_ref[l : l + 1], (HEADS, width)), 0.0) for l in range(LEVELS)],
        0,
    )
    scores = jnp.zeros((rows, LEVELS * HEADS), F32)
    for _ in range(3):
        piece = query.astype(BF)
        scores += lax.dot_general(keys, piece, NT, preferred_element_type=F32)
        query = query - piece.astype(F32)
    scores = (scores * (1.0 / math.sqrt(HD))).reshape(TPS, PATCHES, LEVELS * HEADS)
    top = jnp.max(scores, axis=0)
    expo = jnp.exp(scores - top[None])
    mass = jnp.sum(expo, axis=0)
    expo = expo.reshape(rows, LEVELS * HEADS).astype(BF)
    values = values.reshape(TPS, PATCHES, width)
    parts = []
    for value, count in ((top, 3), (mass, 2)):
        for _ in range(count):
            piece = value.astype(BF)
            parts.append(piece)
            value = value - piece.astype(F32)
    pick = lax.broadcasted_iota(jnp.int32, (LEVELS * HEADS, width), 0)
    stat_row = lax.broadcasted_iota(jnp.int32, (LEVELS * HEADS, FP), 0)
    stat_lane = lax.broadcasted_iota(jnp.int32, (LEVELS * HEADS, FP), 1)
    lane = lax.shift_right_logical(lax.broadcasted_iota(jnp.int32, (LEVELS * HEADS, width), 1), int(math.log2(HD)))
    blocks = []
    for level in range(LEVELS):
        wide = jnp.where(pick == lane + level * HEADS, 1.0, 0.0).astype(BF)
        share = jnp.dot(expo, wide, preferred_element_type=F32).reshape(TPS, PATCHES, width)
        partial = jnp.sum(share * values, axis=0)
        stats = jnp.zeros((PATCHES, FP), F32)
        for n, piece in enumerate(parts):
            to = (stat_row - level * HEADS == stat_lane - n * HEADS) & (stat_row >= level * HEADS) & (stat_row < (level + 1) * HEADS)
            stats += jnp.dot(piece, jnp.where(to, 1.0, 0.0).astype(BF), preferred_element_type=F32)
        blocks.append(jnp.concatenate([partial, stats], 1).astype(BF))
    stacked = jnp.concatenate(blocks, 0)
    count = LEVELS * PATCHES
    target = lax.broadcasted_iota(jnp.int32, (count, count), 0)
    source = lax.broadcasted_iota(jnp.int32, (count, count), 1)
    moved = (target & (LEVELS - 1)) * PATCHES + lax.shift_right_logical(target, 2) == source
    out_ref[...] = jnp.dot(jnp.where(moved, 1.0, 0.0).astype(BF), stacked, preferred_element_type=F32).astype(BF)


def attend(tokens, rows, bias, gain, kv_weight, latents):
    width = kv_weight.shape[0]
    return pl.pallas_call(
        attend_kernel,
        out_shape=jax.ShapeDtypeStruct((PATCHES * LEVELS, width + FP), BF),
        compiler_params=pltpu.CompilerParams(vmem_limit_bytes=KERNEL_VMEM),
        cost_estimate=pl.CostEstimate(flops=2 * 384 * 512 * 4000, bytes_accessed=3000000, transcendentals=12288),
        name="attend_source",
    )(tokens, rows, bias, gain, kv_weight, latents)


def finish_kernel(parts_ref, weight_ref, out_ref):
    sources, rows, wide = parts_ref.shape
    width = wide - FP
    stats = parts_ref[:, :, width:].reshape(sources * rows, FP)
    row = lax.broadcasted_iota(jnp.int32, (FP, width), 0)
    head = lax.shift_right_logical(lax.broadcasted_iota(jnp.int32, (FP, width), 1), int(math.log2(HD)))
    same = (row & (HEADS - 1)) == head
    is_top = jnp.where(same & (row < 3 * HEADS), 1.0, 0.0).astype(BF)
    is_mass = jnp.where(same & (row >= 3 * HEADS) & (row < 5 * HEADS), 1.0, 0.0).astype(BF)
    top = jnp.dot(stats, is_top, preferred_element_type=F32).reshape(sources, rows, width)
    mass = jnp.dot(stats, is_mass, preferred_element_type=F32).reshape(sources, rows, width)
    scale = jnp.exp(top - jnp.max(top, axis=0)[None])
    above = jnp.sum(scale * parts_ref[:, :, :width].astype(F32), axis=0)
    attended = (above / jnp.sum(scale * mass, axis=0)).astype(BF)
    result = jnp.dot(attended, weight_ref[...], preferred_element_type=F32)
    for patch in range(rows // LEVELS):
        out_ref[patch] = result[patch * LEVELS : (patch + 1) * LEVELS]


def finish(parts, out_weight):
    return pl.pallas_call(
        finish_kernel,
        out_shape=jax.ShapeDtypeStruct((parts.shape[1] // LEVELS, LEVELS, out_weight.shape[1]), F32),
        cost_estimate=pl.CostEstimate(flops=2 * 128 * 128 * 1024, bytes_accessed=800000, transcendentals=65536),
        name="combine_sources",
    )(parts, out_weight)


def device_at(y, x, core):
    return ((y % SIDE) * SIDE + x % SIDE) * 2 + core


def shift(offset, second):
    pairs = []
    for y in range(SIDE):
        for x in range(SIDE):
            for core in range(2):
                along_x = (core == 0) != second
                to = device_at(y, x + offset, core) if along_x else device_at(y + offset, x, core)
                pairs.append((device_at(y, x, core), to))
    return pairs


def send(array, offset, second):
    return lax.ppermute(array, "lat", shift(offset, second))


def offset_at(index):
    return jnp.where(index == 0, 0, jnp.where(index == 1, -1, index - 1))


def index_of(offset):
    offset = offset % SIDE
    return jnp.where(offset == 0, 0, jnp.where(offset == SIDE - 1, 1, offset + 1))


def body(
    swath,
    tile_band,
    tile_patch,
    fp_pos,
    conv_weight,
    conv_bias,
    norm_gain,
    latents,
    kv_weight,
    out_weight,
):
    place = lax.axis_index("lat")
    core, chip = place % 2, place // 2
    chip_y, chip_x = chip // SIDE, chip % SIDE
    swath, fp_pos = swath[0], fp_pos[0]
    channels, cols = swath.shape[1], conv_weight.shape[4]
    width = kv_weight.shape[0]
    swap = [(i, i ^ 1) for i in range(2 * CHIPS)]

    shard = jnp.transpose(conv_weight[0].reshape(TAPS, channels, cols), (0, 2, 1))
    center = jnp.asarray(
        np.concatenate([centers(list(range(TPS)) + [-1] * 4), centers([-1] * 4 + list(ROW_TOKEN[TPS:]))], 0)
    )
    half = TAPS // 2
    up, down = send(shard, 1, False), send(shard, -1, False)
    sib_swath = lax.ppermute(swath, "lat", swap)
    sib_pos = lax.ppermute(fp_pos, "lat", swap)
    record = tile_records(tile_band[0, :, 0], tile_patch[0], fp_pos)
    up, down, record = lax.optimization_barrier((up, down, record))
    far = [send(up[:half], 1, False), send(down[half:], -1, False)]
    others = [send(record, -offset, False) for offset in OFFSETS[1:]]
    *far, record, sib_pos, sib_swath = lax.optimization_barrier(
        (*far, jnp.stack([record] + others, 0), sib_pos, sib_swath)
    )
    low = jnp.stack([shard, up], 0)
    high = jnp.stack([down, jnp.concatenate(far, 0)], 0)
    above_low, below_high = send(low, 1, True), send(high, -1, True)
    record = jnp.stack([record] + [send(record, -offset, True) for offset in OFFSETS[1:]], 0)
    above_low, below_high, low, high, record, swath, sib_swath = lax.optimization_barrier(
        (above_low, below_high, low, high, record, swath, sib_swath)
    )
    corner_low, corner_high = send(above_low, 1, True), send(below_high, -1, True)
    above_high, below_low = send(high, 1, True), send(low, -1, True)
    sib_record = lax.ppermute(record, "lat", swap)
    own = gridded(swath, fp_pos, center)
    sib = gridded(sib_swath, sib_pos, center)
    weights = [low, high, above_low, above_high, below_low, below_high, corner_low, corner_high]

    inverse, rows = inverse_density(
        core[None].astype(jnp.int32), record.reshape(-1, RECORD), sib_record.reshape(-1, RECORD)
    )

    column = jnp.arange(CHIPS * cols, dtype=jnp.int32)[None, :]
    near, farther = offset_at(column // cols % SIDE), offset_at(column // cols // SIDE)
    at_y = (chip_y + jnp.where(core == 0, farther, near)) % SIDE
    at_x = (chip_x + jnp.where(core == 0, near, farther)) % SIDE
    columns = (at_y * SIDE + at_x) * cols + column % cols
    outgoing = embed(own, sib, weights, inverse, columns.astype(jnp.int32), rows)

    record, sib_record, conv_bias, norm_gain, kv_weight, outgoing = lax.optimization_barrier(
        (record, sib_record, conv_bias, norm_gain, kv_weight, outgoing)
    )
    about = jnp.stack([record[..., CELLS : CELLS + 2], sib_record[..., CELLS : CELLS + 2]])
    about = about.reshape(2, CHIPS, TILES, 2).astype(F32)
    outgoing = outgoing.reshape(2 * CHIPS, SLOTS * TPS, CHIPS * cols)
    incoming = lax.all_to_all(outgoing, "lat", split_axis=0, concat_axis=0, tiled=True)
    mine = about[..., 0] == place.astype(F32)
    patches = jnp.where(mine, about[..., 1] + 1, 0)
    before = jnp.einsum("cdt,tu->cdu", mine.astype(F32), jnp.asarray(np.triu(np.ones((TILES, TILES), np.float32), 1)))
    patch_at = jnp.stack([jnp.sum(jnp.where(before == n, patches, 0), axis=2) for n in range(2)], 2)
    number = jnp.arange(CHIPS)
    in_y, in_x = index_of(number // SIDE - chip_y), index_of(number % SIDE - chip_x)
    x_first, y_first = SIDE * in_y + in_x, SIDE * in_x + in_y
    order = jnp.stack([jnp.where(core == 0, x_first, y_first), jnp.where(core == 0, y_first, x_first)])
    hot = (order[:, :, None] == number[None, None, :]).astype(F32)
    patch_by = jnp.einsum("cnd,cdk->nck", hot, patch_at)
    patch_by = jnp.where(core == 0, patch_by, patch_by[:, ::-1])
    patch_in = patch_by.astype(jnp.int32).reshape(-1, 1) - 1
    token_in = jnp.where(patch_in < 0, -1, patch_in + PATCHES * jnp.arange(TPS)[None, :]).reshape(1, -1)

    def by_core(array):
        shape = array.shape[1:]
        split = array.reshape((CHIPS, 2, cols) + shape)
        return jnp.swapaxes(split, 0, 1).reshape((width,) + shape)

    parts = attend(
        incoming.reshape(CHIPS, 2, SLOTS * TPS, CHIPS * cols),
        token_in.astype(jnp.int32),
        by_core(conv_bias[0])[None],
        by_core(norm_gain)[None],
        by_core(kv_weight),
        latents,
    )
    sources = lax.axis_size("src")
    parts = lax.all_to_all(
        parts.reshape(sources, -1, width + FP), "src", split_axis=0, concat_axis=0, tiled=True
    )
    return finish(parts, out_weight)


def solution(mesh):
    in_specs = (
        P("src", "lat", None, None),
        P("src", "lat", None),
        P("src", "lat"),
        P("src", "lat", None, None),
        P("src", None, None, None, "lat"),
        P("src", None),
        P(),
        P(),
        P(),
        P(),
    )
    out_specs = P(("lat", "src"), None, None)
    return jax.shard_map(body, mesh=mesh, in_specs=in_specs, out_specs=out_specs, check_vma=False)
```

```python
import math

import jax
import jax.numpy as jnp
import numpy as np
from jax import lax
from jax.experimental import pallas as pl
from jax.experimental.pallas import tpu as pltpu
from jax.sharding import PartitionSpec as P

HEADS = 8
HD = 64
PW = 24
KS = 4
TPS = 12
LEVELS = 4
TILES = 32
PATCHES = 32
CHIPS = 16
SIDE = 4
CELLS = 192
TAPS = KS * KS
SLOTS = 4
FP = 128
PAIR = 2 * TPS
FAR = 1.0e4
OFFSETS = (0, -1, 1, 2)
ROW_TOKEN = np.array(list(range(TPS)) + [8, 9, 10, 11, 0, 1, 2, 3, 4, 5, 6, 7])
BF = jnp.bfloat16
F32 = jnp.float32
NT = (((1,), (1,)), ((), ()))
KERNEL_VMEM = 24 * 2**20
RECORD = 256
STEP = 16
SMALL = pl.CostEstimate(flops=1000000, bytes_accessed=10000, transcendentals=0)


def centers(tokens):
    rows, cols = [], []
    for tap in range(TAPS):
        for token in tokens:
            rows.append(token // 6 * KS + tap // KS + 0.5 if token >= 0 else FAR)
            cols.append(token % 6 * KS + tap % KS + 0.5 if token >= 0 else FAR)
    wide = [np.repeat(np.array(v, np.float32)[:, None], FP, 1) for v in (rows, cols)]
    return np.stack(wide)


def weights_at(pos, center_ref, index):
    down = pos[0:1] - center_ref[index]
    across = pos[1:2] - center_ref[index + 1]
    return jnp.exp((down * down + across * across) * (-1.0 / 1.125))


def record_kernel(band_ref, patch_ref, pos_ref, center_ref, out_ref):
    ones = jnp.ones((8, FP), BF)
    place = lax.broadcasted_iota(jnp.int32, (8, RECORD), 0)
    lane = lax.broadcasted_iota(jnp.int32, (8, RECORD - CELLS), 1)

    def group(g, carry):
        base = pl.multiple_of(g * 8, 8)
        total = jnp.zeros((8, RECORD), F32)
        for j in range(8):
            table = weights_at(pos_ref[base + j].astype(F32), center_ref, 0).astype(BF)
            row = lax.dot_general(ones, table, NT, preferred_element_type=F32)
            about = jnp.where(lane == 0, band_ref[base + j], patch_ref[base + j]).astype(F32)
            total = jnp.where(place == j, jnp.concatenate([row, about], 1), total)
        return carry + (total,)

    rows = ()
    for g in range(TILES // 8):
        rows = group(g, rows)
    out_ref[...] = jnp.concatenate(rows, 0).astype(BF)


def tile_records(band, patch, pos):
    vmem, smem = pl.BlockSpec(memory_space=pltpu.VMEM), pl.BlockSpec(memory_space=pltpu.SMEM)
    return pl.pallas_call(
        record_kernel,
        in_specs=[smem, smem, vmem, vmem],
        out_shape=jax.ShapeDtypeStruct((TILES, RECORD), BF),
        cost_estimate=SMALL,
        name="tile_records",
    )(band, patch, pos, jnp.asarray(centers(range(TPS))))


def inverse_kernel(core_ref, own_ref, sib_ref, token_ref, row_tile_ref, own_cell_ref, tap_ref, out_ref, row_ref):
    here = 2 * TILES

    def as_row(column):
        return jnp.broadcast_to(column, (column.shape[0], FP)).T[:1]

    about = jnp.concatenate([own_ref[:TILES, CELLS:], sib_ref[:TILES, CELLS:]], 0).astype(F32)
    band, target = about[:, :1], about[:, :1] * PATCHES + about[:, 1:2]
    band_row, target_row = as_row(band), as_row(target)
    total = jnp.ones((CELLS, here), F32)
    for ref in (own_ref, sib_ref):
        about = ref[:, CELLS:].astype(F32)
        same = jnp.where(about[:, :1] * PATCHES + about[:, 1:2] == target_row, 1.0, 0.0).astype(BF)
        total += lax.dot_general(ref[:, :CELLS], same, (((0,), (0,)), ((), ())), preferred_element_type=F32)
    inverse = 1.0 / total
    out = jnp.zeros(out_ref.shape, F32)
    for _ in range(3):
        piece = inverse.astype(BF)
        spread = jnp.dot(piece, row_tile_ref[...], preferred_element_type=F32).astype(BF) * own_cell_ref[...]
        out += jnp.dot(tap_ref[...], spread, preferred_element_type=F32)
        inverse = inverse - piece.astype(F32)
    out_ref[...] = out
    other = lax.broadcasted_iota(jnp.int32, (here, here), 0)
    tile = lax.broadcasted_iota(jnp.int32, (here, here), 1)
    earlier = (other < tile) & ((other < TILES) == (tile < TILES)) & (band == band_row)
    rank = jnp.sum(jnp.where(earlier, 1.0, 0.0), axis=0, keepdims=True)
    origin = jnp.where(tile[:1] < TILES, core_ref[0], 1 - core_ref[0]).astype(F32)
    slots = jnp.broadcast_to(band_row * SLOTS + 2 * origin + rank, (8, here)).astype(BF)
    slots = jnp.dot(slots, row_tile_ref[...], preferred_element_type=F32)
    row_ref[...] = slots[:1].astype(jnp.int32) * TPS + token_ref[...]


def inverse_density(core, own, sib):
    rows = 2 * TILES * TPS
    row_tile = (np.arange(2 * TILES)[:, None] == np.arange(rows)[None, :] // TPS).astype(np.float32)
    token = np.tile(ROW_TOKEN, TILES)
    own_cell = (np.arange(CELLS)[:, None] % TPS == token[None, :]).astype(np.float32)
    tap = (np.arange(TAPS)[:, None] == np.arange(CELLS)[None, :] // TPS).astype(np.float32)
    vmem, smem = pl.BlockSpec(memory_space=pltpu.VMEM), pl.BlockSpec(memory_space=pltpu.SMEM)
    return pl.pallas_call(
        inverse_kernel,
        in_specs=[smem] + [vmem] * 6,
        out_shape=(jax.ShapeDtypeStruct((TAPS, rows), F32), jax.ShapeDtypeStruct((1, rows), jnp.int32)),
        compiler_params=pltpu.CompilerParams(vmem_limit_bytes=KERNEL_VMEM // 2),
        cost_estimate=SMALL,
        name="inverse_density",
    )(core, own, sib, jnp.asarray(token, jnp.int32)[None], *(jnp.asarray(v, BF) for v in (row_tile, own_cell, tap)))


def grid_kernel(swath_ref, pos_ref, center_ref, out_ref):
    channels = swath_ref.shape[1]
    gap = jnp.zeros((TAPS, 8, FP), F32)

    def step(tiles_ref):
        i = pl.program_id(0)
        for quad in range(STEP // 4):
            blocks = []
            for pair in range(2):
                place = 4 * quad + 2 * pair
                first, second = STEP * i + place, STEP * i + place + 1
                left = weights_at(pos_ref[first].astype(F32), center_ref, 0).reshape(TAPS, 16, FP)
                right = weights_at(pos_ref[second].astype(F32), center_ref, 2).reshape(TAPS, 16, FP)
                left = jnp.concatenate([left, gap], 1).reshape(TAPS * PAIR, FP)
                right = jnp.concatenate([gap, right], 1).reshape(TAPS * PAIR, FP)
                table = jnp.concatenate([left, right], 1).astype(BF)
                data = jnp.concatenate([tiles_ref[place], tiles_ref[place + 1]], 1)
                total = lax.dot_general(table, data, NT, preferred_element_type=F32)
                blocks.append(total.reshape(TAPS, PAIR, channels))
            base = pl.multiple_of((STEP // 4 * i + quad) * 2 * PAIR, 2 * PAIR)
            out_ref[:, pl.ds(base, 2 * PAIR), :] = jnp.concatenate(blocks, 1).astype(BF)

    pltpu.emit_pipeline(
        step, grid=(TILES // STEP,), in_specs=[pl.BlockSpec((STEP, channels, FP), lambda i: (i, 0, 0))]
    )(swath_ref)


def gridded(swath, pos, center):
    channels = swath.shape[1]
    vmem = pl.BlockSpec(memory_space=pltpu.VMEM)
    swath = pltpu.with_memory_space_constraint(swath, pltpu.HBM)
    return pl.pallas_call(
        grid_kernel,
        in_specs=[pl.BlockSpec(memory_space=pl.ANY), vmem, vmem],
        out_specs=vmem,
        out_shape=pltpu.VMEM((TAPS, TILES * TPS, channels), BF),
        compiler_params=pltpu.CompilerParams(vmem_limit_bytes=KERNEL_VMEM // 2),
        cost_estimate=SMALL,
        name="grid_tiles",
    )(swath, pos, center)


def embed_kernel(own_ref, sib_ref, *refs):
    *weight_refs, inverse_ref, column_ref, row_ref, out_ref, total, spread = refs
    channels = own_ref.shape[2]
    slot_rows, half = out_ref.shape[0], own_ref.shape[1]
    part = slot_rows // TAPS
    width = total.shape[1]
    total[...] = jnp.zeros_like(total)

    def tap(k, carry):
        weight = jnp.concatenate([w[:, k].reshape(-1, channels) for w in weight_refs], 0)
        scale = jnp.broadcast_to(inverse_ref[pl.ds(k, 1), :], (FP, 2 * half)).T
        scale = jnp.concatenate([scale] * (width // FP), 1)
        for n, ref in enumerate((own_ref, sib_ref)):
            rows = slice(n * half, (n + 1) * half)
            product = lax.dot_general(ref[k], weight, NT, preferred_element_type=F32)
            total[rows] += product * scale[rows]
        base = pl.multiple_of(k * part, part)
        here = lax.broadcasted_iota(jnp.int32, (part, 2 * half), 0) + base
        spread[pl.ds(base, part), :] = jnp.where(here == row_ref[...], 1.0, 0.0).astype(BF)
        return carry

    lax.fori_loop(0, TAPS, tap, 0, unroll=8)
    columns = lax.broadcasted_iota(jnp.int32, (width, width), 0)
    order = jnp.where(columns == column_ref[...], 1.0, 0.0).astype(BF)
    tokens = lax.dot_general(total[...].astype(BF), order, NT, preferred_element_type=F32).astype(BF)
    out_ref[...] = jnp.dot(spread[...], tokens, preferred_element_type=F32).astype(BF)


def embed(own, sib, weights, inverse, columns, rows):
    width = CHIPS * weights[0].shape[2]
    slot_rows = 2 * CHIPS * SLOTS * TPS
    half = TILES * TPS
    vmem = pl.BlockSpec(memory_space=pltpu.VMEM)
    large = [pltpu.with_memory_space_constraint(a, pltpu.VMEM) for a in (own, sib, *weights)]
    return pl.pallas_call(
        embed_kernel,
        in_specs=[vmem] * (len(large) + 3),
        out_specs=vmem,
        out_shape=jax.ShapeDtypeStruct((slot_rows, width), BF),
        scratch_shapes=[pltpu.VMEM((2 * half, width), F32), pltpu.VMEM((slot_rows, 2 * half), BF)],
        compiler_params=pltpu.CompilerParams(vmem_limit_bytes=KERNEL_VMEM // 2),
        cost_estimate=pl.CostEstimate(flops=2 * TAPS * 2 * half * 768 * width * 2, bytes_accessed=1000000, transcendentals=0),
        name="embed_tiles",
    )(*large, inverse, columns, rows)


def attend_kernel(tokens_ref, row_ref, bias_ref, gain_ref, kv_ref, latent_ref, out_ref):
    rows = TPS * PATCHES
    per_core = tokens_ref.shape[0] * tokens_ref.shape[2]
    width = 2 * tokens_ref.shape[3]
    hot = lax.broadcasted_iota(jnp.int32, (rows, per_core), 0) == row_ref[...]
    hot = jnp.where(hot, 1.0, 0.0).astype(BF)
    halves = [
        jnp.dot(hot, tokens_ref[:, c].reshape(per_core, width // 2), preferred_element_type=F32) for c in range(2)
    ]
    tokens = (jnp.concatenate(halves, 1) + bias_ref[...]).astype(BF).astype(F32)
    mean = jnp.mean(tokens, axis=1, keepdims=True)
    shifted = tokens - mean
    var = jnp.mean(shifted * shifted, axis=1, keepdims=True)
    normed = (shifted * lax.rsqrt(var + 1e-05) * gain_ref[...]).astype(BF)
    keys_values = jnp.dot(normed, kv_ref[...], preferred_element_type=F32).astype(BF)
    keys, values = keys_values[:, :width], keys_values[:, width:].astype(F32)
    head = lax.broadcasted_iota(jnp.int32, (HEADS, width), 0)
    lane_head = lax.shift_right_logical(lax.broadcasted_iota(jnp.int32, (HEADS, width), 1), int(math.log2(HD)))
    query = jnp.concatenate(
        [jnp.where(head == lane_head, jnp.broadcast_to(latent_ref[l : l + 1], (HEADS, width)), 0.0) for l in range(LEVELS)],
        0,
    )
    scores = jnp.zeros((rows, LEVELS * HEADS), F32)
    for _ in range(3):
        piece = query.astype(BF)
        scores += lax.dot_general(keys, piece, NT, preferred_element_type=F32)
        query = query - piece.astype(F32)
    scores = (scores * (1.0 / math.sqrt(HD))).reshape(TPS, PATCHES, LEVELS * HEADS)
    top = jnp.max(scores, axis=0)
    expo = jnp.exp(scores - top[None])
    mass = jnp.sum(expo, axis=0)
    expo = expo.reshape(rows, LEVELS * HEADS).astype(BF)
    values = values.reshape(TPS, PATCHES, width)
    parts = []
    for value, count in ((top, 3), (mass, 2)):
        for _ in range(count):
            piece = value.astype(BF)
            parts.append(piece)
            value = value - piece.astype(F32)
    pick = lax.broadcasted_iota(jnp.int32, (LEVELS * HEADS, width), 0)
    stat_row = lax.broadcasted_iota(jnp.int32, (LEVELS * HEADS, FP), 0)
    stat_lane = lax.broadcasted_iota(jnp.int32, (LEVELS * HEADS, FP), 1)
    lane = lax.shift_right_logical(lax.broadcasted_iota(jnp.int32, (LEVELS * HEADS, width), 1), int(math.log2(HD)))
    blocks = []
    for level in range(LEVELS):
        wide = jnp.where(pick == lane + level * HEADS, 1.0, 0.0).astype(BF)
        share = jnp.dot(expo, wide, preferred_element_type=F32).reshape(TPS, PATCHES, width)
        partial = jnp.sum(share * values, axis=0)
        stats = jnp.zeros((PATCHES, FP), F32)
        for n, piece in enumerate(parts):
            to = (stat_row - level * HEADS == stat_lane - n * HEADS) & (stat_row >= level * HEADS) & (stat_row < (level + 1) * HEADS)
            stats += jnp.dot(piece, jnp.where(to, 1.0, 0.0).astype(BF), preferred_element_type=F32)
        blocks.append(jnp.concatenate([partial, stats], 1).astype(BF))
    stacked = jnp.concatenate(blocks, 0)
    count = LEVELS * PATCHES
    target = lax.broadcasted_iota(jnp.int32, (count, count), 0)
    source = lax.broadcasted_iota(jnp.int32, (count, count), 1)
    moved = (target & (LEVELS - 1)) * PATCHES + lax.shift_right_logical(target, 2) == source
    out_ref[...] = jnp.dot(jnp.where(moved, 1.0, 0.0).astype(BF), stacked, preferred_element_type=F32).astype(BF)


def attend(tokens, rows, bias, gain, kv_weight, latents):
    width = kv_weight.shape[0]
    return pl.pallas_call(
        attend_kernel,
        out_shape=jax.ShapeDtypeStruct((PATCHES * LEVELS, width + FP), BF),
        compiler_params=pltpu.CompilerParams(vmem_limit_bytes=KERNEL_VMEM),
        cost_estimate=pl.CostEstimate(flops=2 * 384 * 512 * 4000, bytes_accessed=3000000, transcendentals=12288),
        name="attend_source",
    )(tokens, rows, bias, gain, kv_weight, latents)


def finish_kernel(parts_ref, weight_ref, out_ref):
    sources, rows, wide = parts_ref.shape
    width = wide - FP
    stats = parts_ref[:, :, width:].reshape(sources * rows, FP)
    row = lax.broadcasted_iota(jnp.int32, (FP, width), 0)
    head = lax.shift_right_logical(lax.broadcasted_iota(jnp.int32, (FP, width), 1), int(math.log2(HD)))
    same = (row & (HEADS - 1)) == head
    is_top = jnp.where(same & (row < 3 * HEADS), 1.0, 0.0).astype(BF)
    is_mass = jnp.where(same & (row >= 3 * HEADS) & (row < 5 * HEADS), 1.0, 0.0).astype(BF)
    top = jnp.dot(stats, is_top, preferred_element_type=F32).reshape(sources, rows, width)
    mass = jnp.dot(stats, is_mass, preferred_element_type=F32).reshape(sources, rows, width)
    scale = jnp.exp(top - jnp.max(top, axis=0)[None])
    above = jnp.sum(scale * parts_ref[:, :, :width].astype(F32), axis=0)
    attended = (above / jnp.sum(scale * mass, axis=0)).astype(BF)
    result = jnp.dot(attended, weight_ref[...], preferred_element_type=F32)
    for patch in range(rows // LEVELS):
        out_ref[patch] = result[patch * LEVELS : (patch + 1) * LEVELS]


def finish(parts, out_weight):
    return pl.pallas_call(
        finish_kernel,
        out_shape=jax.ShapeDtypeStruct((parts.shape[1] // LEVELS, LEVELS, out_weight.shape[1]), F32),
        cost_estimate=pl.CostEstimate(flops=2 * 128 * 128 * 1024, bytes_accessed=800000, transcendentals=65536),
        name="combine_sources",
    )(parts, out_weight)


def device_at(y, x, core):
    return ((y % SIDE) * SIDE + x % SIDE) * 2 + core


def shift(offset, second):
    pairs = []
    for y in range(SIDE):
        for x in range(SIDE):
            for core in range(2):
                along_x = (core == 0) != second
                to = device_at(y, x + offset, core) if along_x else device_at(y + offset, x, core)
                pairs.append((device_at(y, x, core), to))
    return pairs


def send(array, offset, second):
    return lax.ppermute(array, "lat", shift(offset, second))


def offset_at(index):
    return jnp.where(index == 0, 0, jnp.where(index == 1, -1, index - 1))


def index_of(offset):
    offset = offset % SIDE
    return jnp.where(offset == 0, 0, jnp.where(offset == SIDE - 1, 1, offset + 1))


def body(
    swath,
    tile_band,
    tile_patch,
    fp_pos,
    conv_weight,
    conv_bias,
    norm_gain,
    latents,
    kv_weight,
    out_weight,
):
    place = lax.axis_index("lat")
    core, chip = place % 2, place // 2
    chip_y, chip_x = chip // SIDE, chip % SIDE
    swath, fp_pos = swath[0], fp_pos[0]
    channels, cols = swath.shape[1], conv_weight.shape[4]
    width = kv_weight.shape[0]
    swap = [(i, i ^ 1) for i in range(2 * CHIPS)]

    shard = jnp.transpose(conv_weight[0].reshape(TAPS, channels, cols), (0, 2, 1))
    center = jnp.asarray(
        np.concatenate([centers(list(range(TPS)) + [-1] * 4), centers([-1] * 4 + list(ROW_TOKEN[TPS:]))], 0)
    )
    half = TAPS // 2
    up, down = send(shard, 1, False), send(shard, -1, False)
    sib_swath = lax.ppermute(swath, "lat", swap)
    sib_pos = lax.ppermute(fp_pos, "lat", swap)
    record = tile_records(tile_band[0, :, 0], tile_patch[0], fp_pos)
    up, down = lax.optimization_barrier((up, down))
    far = [send(up[:half], 1, False), send(down[half:], -1, False)]
    others = [send(record, -offset, False) for offset in OFFSETS[1:]]
    *far, record, sib_pos, sib_swath = lax.optimization_barrier(
        (*far, jnp.stack([record] + others, 0), sib_pos, sib_swath)
    )
    low = jnp.stack([shard, up], 0)
    high = jnp.stack([down, jnp.concatenate(far, 0)], 0)
    above_low, below_high = send(low, 1, True), send(high, -1, True)
    record = jnp.stack([record] + [send(record, -offset, True) for offset in OFFSETS[1:]], 0)
    above_low, below_high, low, high, record, swath, sib_swath = lax.optimization_barrier(
        (above_low, below_high, low, high, record, swath, sib_swath)
    )
    corner_low, corner_high = send(above_low, 1, True), send(below_high, -1, True)
    above_high, below_low = send(high, 1, True), send(low, -1, True)
    sib_record = lax.ppermute(record, "lat", swap)
    own = gridded(swath, fp_pos, center)
    sib = gridded(sib_swath, sib_pos, center)
    weights = [low, high, above_low, above_high, below_low, below_high, corner_low, corner_high]

    inverse, rows = inverse_density(
        core[None].astype(jnp.int32), record.reshape(-1, RECORD), sib_record.reshape(-1, RECORD)
    )

    column = jnp.arange(CHIPS * cols, dtype=jnp.int32)[None, :]
    near, farther = offset_at(column // cols % SIDE), offset_at(column // cols // SIDE)
    at_y = (chip_y + jnp.where(core == 0, farther, near)) % SIDE
    at_x = (chip_x + jnp.where(core == 0, near, farther)) % SIDE
    columns = (at_y * SIDE + at_x) * cols + column % cols
    outgoing = embed(own, sib, weights, inverse, columns.astype(jnp.int32), rows)

    record, sib_record, conv_bias, norm_gain, kv_weight, outgoing = lax.optimization_barrier(
        (record, sib_record, conv_bias, norm_gain, kv_weight, outgoing)
    )
    about = jnp.stack([record[..., CELLS : CELLS + 2], sib_record[..., CELLS : CELLS + 2]])
    about = about.reshape(2, CHIPS, TILES, 2).astype(F32)
    outgoing = outgoing.reshape(2 * CHIPS, SLOTS * TPS, CHIPS * cols)
    incoming = lax.all_to_all(outgoing, "lat", split_axis=0, concat_axis=0, tiled=True)
    mine = about[..., 0] == place.astype(F32)
    patches = jnp.where(mine, about[..., 1] + 1, 0)
    before = jnp.einsum("cdt,tu->cdu", mine.astype(F32), jnp.asarray(np.triu(np.ones((TILES, TILES), np.float32), 1)))
    patch_at = jnp.stack([jnp.sum(jnp.where(before == n, patches, 0), axis=2) for n in range(2)], 2)
    number = jnp.arange(CHIPS)
    in_y, in_x = index_of(number // SIDE - chip_y), index_of(number % SIDE - chip_x)
    x_first, y_first = SIDE * in_y + in_x, SIDE * in_x + in_y
    order = jnp.stack([jnp.where(core == 0, x_first, y_first), jnp.where(core == 0, y_first, x_first)])
    hot = (order[:, :, None] == number[None, None, :]).astype(F32)
    patch_by = jnp.einsum("cnd,cdk->nck", hot, patch_at)
    patch_by = jnp.where(core == 0, patch_by, patch_by[:, ::-1])
    patch_in = patch_by.astype(jnp.int32).reshape(-1, 1) - 1
    token_in = jnp.where(patch_in < 0, -1, patch_in + PATCHES * jnp.arange(TPS)[None, :]).reshape(1, -1)

    def by_core(array):
        shape = array.shape[1:]
        split = array.reshape((CHIPS, 2, cols) + shape)
        return jnp.swapaxes(split, 0, 1).reshape((width,) + shape)

    parts = attend(
        incoming.reshape(CHIPS, 2, SLOTS * TPS, CHIPS * cols),
        token_in.astype(jnp.int32),
        by_core(conv_bias[0])[None],
        by_core(norm_gain)[None],
        by_core(kv_weight),
        latents,
    )
    sources = lax.axis_size("src")
    parts = lax.all_to_all(
        parts.reshape(sources, -1, width + FP), "src", split_axis=0, concat_axis=0, tiled=True
    )
    return finish(parts, out_weight)


def solution(mesh):
    in_specs = (
        P("src", "lat", None, None),
        P("src", "lat", None),
        P("src", "lat"),
        P("src", "lat", None, None),
        P("src", None, None, None, "lat"),
        P("src", None),
        P(),
        P(),
        P(),
        P(),
    )
    out_specs = P(("lat", "src"), None, None)
    return jax.shard_map(body, mesh=mesh, in_specs=in_specs, out_specs=out_specs, check_vma=False)
```
